32 devices in a mesh: dom: 8 (over y, x, core), feat: 4 (over z).
Axes of the slice: x: 2, y: 2, z: 4, core: 2. Of those that a mesh axis runs over, the one named last changes fastest.
Arguments:
- state: bfloat16 [512, 16384], P('feat', 'dom'), may hold values from -3 to 3
- inputs: bfloat16 [2, 16384], P(None, 'dom'), may hold values from -6 to 6
- adj_tiles: bfloat16 [128, 4, 128, 128], P('dom'), may hold values from -0.25 to 0.25
- adj_cols: int32 [128, 4], P('dom'), may hold values from 0 to 17, as said below
- valid_rows: int32 [8], P('dom'), may hold values from 1024 to 2048, as said below
- cluster_of: int32 [16384], P('dom'), may hold values from 0 to 2047
- w_gates: bfloat16 [3, 512, 4, 512], P(None, 'feat'), may hold values from -0.125 to 0.125
- w_input: bfloat16 [3, 512, 2], P(None, 'feat'), may hold values from -4 to 4
- bias: float32 [3, 512], P(None, 'feat'), may hold values from -4 to 4
- w_value: bfloat16 [8, 64, 64], P('feat'), may hold values from -0.75 to 0.75
- source_emb: float32 [8, 10, 2048], P('feat'), may hold values from -5 to 5
- target_emb: float32 [8, 10, 2048], P('feat'), may hold values from -5 to 5
- coarse_tiles: bfloat16 [16, 2, 128, 128], replicated, may hold values from -0.375 to 0.375
- coarse_cols: int32 [16, 2], replicated, may hold values from 0 to 15
Outputs:
- new_state: bfloat16 [512, 16384], P('feat', 'dom')
The draws below stay inside these ranges and needn't reach their ends.
Inputs may be any that keep to these rules, and one draw needn't show every extreme that they name: `adj_cols`: for local row tile t of a partition (t counted from 0 in the partition), every entry lies in t to t + 2, the first is t and the last is t + 2. `valid_rows`: some partition has all 2048 rows valid and another exactly half of them.
All inputs are finite; a program needn't handle non-finite values.
Results may differ from the reference program's by a relative error of at most 0.003.
Values may be sent and summed in bfloat16 or wider, within the bound.
No kernel may reach another device: no remote copies, remote signals or barrier semaphores. Data moves between devices by JAX's collectives and lax.ppermute only.
A program may use at most 64 MiB of HBM per device.

```python
import math
import jax
import jax.numpy as jnp
from jax import lax

H = 512
HEAD = 64
HEADS = 8
EMB = 10
F_IN = 2
TILE = 128
KB = 4
KC = 2
ROWS_DEV = 2048
SENSORS = 16384
CLUSTERS = 2048
N_DOM = 8


def embed_pair(key):
    base_key = jax.random.fold_in(key, 7001)
    key_source, key_target = jax.random.split(base_key, 2)
    shape = (HEADS, EMB, CLUSTERS)
    source = jnp.clip(jax.random.normal(key_source, shape, jnp.float32), -4.0, 4.0)
    target = jnp.clip(jax.random.normal(key_target, shape, jnp.float32), -4.0, 4.0)
    return (source, target)


def draw_source_emb(key, part):
    return embed_pair(key)[0]


def draw_target_emb(key, part):
    return embed_pair(key)[1]


def draw_adj_cols(key, part):
    tile_rows = SENSORS // TILE
    per_part = ROWS_DEV // TILE
    local_tile = jnp.arange(tile_rows, dtype=jnp.int32) % per_part
    offsets = jax.random.randint(jax.random.fold_in(key, 7002), (tile_rows, KB), 0, 3, dtype=jnp.int32)
    offsets = offsets.at[:, 0].set(0)
    offsets = offsets.at[:, KB - 1].set(2)
    return (local_tile[:, None] + offsets).astype(jnp.int32)


def draw_valid_rows(key, part):
    parts = SENSORS // ROWS_DEV
    key_rows, key_full, key_half = jax.random.split(jax.random.fold_in(key, 7003), 3)
    counts = jax.random.randint(key_rows, (parts,), ROWS_DEV // 2, ROWS_DEV + 1, dtype=jnp.int32)
    full_part = jax.random.randint(key_full, (), 0, parts, dtype=jnp.int32)
    half_part = (full_part + 1 + jax.random.randint(key_half, (), 0, parts - 1, dtype=jnp.int32)) % parts
    counts = counts.at[full_part].set(ROWS_DEV)
    counts = counts.at[half_part].set(ROWS_DEV // 2)
    return counts.astype(jnp.int32)


def place_ends(values, own_key, low, high):
    extent = values.shape
    spot = [jax.random.randint(jax.random.fold_in(own_key, axis), (), 0, extent[axis]) for axis in range(len(extent))]
    values = values.at[tuple(spot)].set(low)
    longest = extent.index(max(extent))
    spot[longest] = (spot[longest] + 1) % extent[longest]
    return values.at[tuple(spot)].set(high)


def block_levels(rng, extent, pieces, low, largest):
    def one(axis_at, shards_of):
        steps = jax.random.uniform(jax.random.fold_in(jax.random.fold_in(rng, 6), axis_at), (shards_of,), jnp.float32, low / len(pieces), largest / len(pieces))
        return jnp.repeat(jnp.exp(steps), extent[axis_at] // shards_of).reshape((-1,) + (1,) * (len(extent) - axis_at - 1))

    gain = one(*pieces[0])
    for cut in pieces[1:]:
        gain = gain * one(*cut)
    return gain


def bell_draw(own_key, shape, width, limit, pieces=(), held_as=jnp.bfloat16):
    values = width * jax.random.normal(own_key, shape, jnp.float32)
    if pieces:
        values = values * block_levels(own_key, shape, pieces, -0.22, 0.18)
    return jnp.clip(values, -limit, limit).astype(held_as)


def setup_inputs(seed: int = 0) -> dict:
    splits = jax.random.split(jax.random.key(seed), 15)
    state = bell_draw(splits[0], (H, SENSORS), 0.5, 3.0, ((0, 4), (1, 8)))
    inputs = bell_draw(splits[1], (F_IN, SENSORS), 1.0, 6.0, ((1, 8),))
    adj_tiles = bell_draw(splits[2], (SENSORS // TILE, KB, TILE, TILE), (KB * TILE) ** -0.5, 0.25, ((0, 8),))
    adj_cols = draw_adj_cols(jax.random.fold_in(splits[14], 71), 0)
    valid_rows = draw_valid_rows(jax.random.fold_in(splits[14], 71), 0)
    cluster_of = place_ends(jax.random.randint(splits[5], (SENSORS,), 0, CLUSTERS), jax.random.fold_in(splits[5], 1), 0, CLUSTERS - 1).astype(jnp.int32)
    w_gates = bell_draw(splits[6], (3, H, 4, H), (4 * H) ** -0.5, 0.125, ((1, 4),))
    w_input = bell_draw(splits[7], (3, H, F_IN), F_IN ** -0.5, 4.0, ((1, 4),))
    bias = bell_draw(splits[8], (3, H), 1.0, 4.0, ((1, 4),), jnp.float32)
    w_value = bell_draw(splits[9], (HEADS, HEAD, HEAD), HEAD ** -0.5, 0.75, ((0, 4),))
    source_emb = draw_source_emb(jax.random.fold_in(splits[14], 71), 0)
    target_emb = draw_target_emb(jax.random.fold_in(splits[14], 71), 0)
    coarse_tiles = bell_draw(splits[12], (CLUSTERS // TILE, KC, TILE, TILE), (KC * TILE) ** -0.5, 0.375)
    coarse_cols = place_ends(jax.random.randint(splits[13], (CLUSTERS // TILE, KC), 0, CLUSTERS // TILE), jax.random.fold_in(splits[13], 1), 0, (CLUSTERS // TILE) - 1).astype(jnp.int32)
    return dict(state=state, inputs=inputs, adj_tiles=adj_tiles, adj_cols=adj_cols, valid_rows=valid_rows, cluster_of=cluster_of, w_gates=w_gates, w_input=w_input, bias=bias, w_value=w_value, source_emb=source_emb, target_emb=target_emb, coarse_tiles=coarse_tiles, coarse_cols=coarse_cols)


def pick_tiles(extended, columns):
    return extended[:, columns]


def diffuse(states, adj_tiles, adj_cols, row_mask):
    tile_count = ROWS_DEV // TILE
    grouped = states.reshape(H, N_DOM, ROWS_DEV)
    before = jnp.roll(grouped, 1, axis=1)[:, :, ROWS_DEV - TILE:]
    after = jnp.roll(grouped, -1, axis=1)[:, :, :TILE]
    extended = jnp.concatenate([before, grouped, after], axis=2)
    extended = extended.reshape(H, N_DOM, tile_count + 2, TILE)
    columns = adj_cols.reshape(N_DOM, tile_count, KB)
    picked = jax.vmap(pick_tiles, in_axes=(1, 0), out_axes=1)(extended, columns)
    tiles = adj_tiles.reshape(N_DOM, tile_count, KB, TILE, TILE)
    result = jnp.einsum("hpnkj,pnkji->hpni", picked.astype(jnp.float32), tiles.astype(jnp.float32))
    return (result.reshape(H, SENSORS) * row_mask).astype(jnp.bfloat16)


def attend(source_emb, target_emb, values):
    heads_here, emb_dim, query_count = source_emb.shape
    block_rows = math.gcd(query_count, 512)
    blocks = source_emb.reshape(heads_here, emb_dim, query_count // block_rows, block_rows)
    blocks = jnp.moveaxis(blocks, 2, 0)

    def one_block(source_block):
        scores = jnp.einsum("hei,hej->hij", source_block, target_emb, precision=lax.Precision.HIGHEST)
        scores = jnp.maximum(scores, 0.0)
        row_peak = jnp.max(scores, axis=2, keepdims=True)
        raised = jnp.exp(scores - row_peak)
        weights = (raised / jnp.sum(raised, axis=2, keepdims=True)).astype(jnp.bfloat16)
        return jnp.einsum("hdj,hij->hdi", values.astype(jnp.float32), weights.astype(jnp.float32))

    outputs = lax.map(one_block, blocks)
    outputs = jnp.moveaxis(outputs, 0, 2)
    return outputs.reshape(heads_here, values.shape[1], query_count)


def reference(state, inputs, adj_tiles, adj_cols, valid_rows, cluster_of, w_gates, w_input, bias, w_value, source_emb, target_emb, coarse_tiles, coarse_cols):
    position = jnp.arange(SENSORS, dtype=jnp.int32)
    partition = position // ROWS_DEV
    local_row = position % ROWS_DEV
    row_mask = (local_row < valid_rows[partition]).astype(jnp.float32)
    masked = (state.astype(jnp.float32) * row_mask).astype(jnp.bfloat16)
    hop_one = diffuse(masked, adj_tiles, adj_cols, row_mask)
    hop_two = diffuse(hop_one, adj_tiles, adj_cols, row_mask)
    cluster_sums = jax.ops.segment_sum(masked.astype(jnp.float32).T, cluster_of, CLUSTERS).T
    counts = jax.ops.segment_sum(row_mask, cluster_of, CLUSTERS)
    pooled = cluster_sums / jnp.maximum(counts, 1.0)[None, :]
    grouped = pooled.reshape(HEADS, HEAD, CLUSTERS)
    values = jnp.einsum("hde,hec->hdc", w_value.astype(jnp.float32), grouped, precision=lax.Precision.HIGHEST).astype(jnp.bfloat16)
    attended = attend(source_emb, target_emb, values).reshape(H, CLUSTERS)
    coarse_attn = (pooled + attended).astype(jnp.bfloat16)
    coarse_grid = coarse_attn.reshape(H, CLUSTERS // TILE, TILE)
    picked = coarse_grid[:, coarse_cols]
    coarse_terms = jnp.einsum("hnkj,nkji->hni", picked.astype(jnp.float32), coarse_tiles.astype(jnp.float32))
    coarse = (coarse_attn.astype(jnp.float32) + coarse_terms.reshape(H, CLUSTERS)).astype(jnp.bfloat16)
    unpooled = jnp.take(coarse, cluster_of, axis=1)
    features = jnp.stack([masked, hop_one, hop_two, unpooled]).astype(jnp.float32)
    gate_sums = jnp.einsum("ghkc,kcs->ghs", w_gates.astype(jnp.float32), features)
    input_terms = jnp.einsum("ghf,fs->ghs", w_input.astype(jnp.float32), inputs.astype(jnp.float32)) + bias[:, :, None]
    update = jax.nn.sigmoid(input_terms[0] + gate_sums[0])
    reset = jax.nn.sigmoid(input_terms[1] + gate_sums[1])
    candidate = jnp.tanh(input_terms[2] + reset * gate_sums[2])
    fresh_state = (update * masked.astype(jnp.float32) + (1.0 - update) * candidate) * row_mask
    return fresh_state.astype(jnp.bfloat16)
```

```python
import functools

import jax
import jax.numpy as jnp
from jax import lax
from jax.experimental import pallas as pl
from jax.experimental.pallas import tpu as pltpu
from jax.sharding import PartitionSpec as P

BF = jnp.bfloat16
F32 = jnp.float32
VMEM = pl.BlockSpec(memory_space=pltpu.VMEM)
SMEM = pl.BlockSpec(memory_space=pltpu.SMEM)
COUNT_ROWS = 16


def call(kernel, outs, ins, scratch=(), flops=0, bytes_accessed=0, mib=40):
    specs = [SMEM if x.dtype == jnp.int32 and x.ndim == 1 else VMEM for x in ins]
    return pl.pallas_call(
        kernel,
        out_shape=outs,
        in_specs=specs,
        out_specs=jax.tree.map(lambda _: VMEM, outs),
        scratch_shapes=list(scratch),
        compiler_params=pltpu.CompilerParams(vmem_limit_bytes=mib * 2**20),
        cost_estimate=pl.CostEstimate(
            flops=int(flops), bytes_accessed=int(bytes_accessed), transcendentals=0
        ),
    )(*ins)


def one_hot(ids, first, width):
    rel = jnp.clip(ids - first, -1, width).astype(F32).astype(BF)
    rows = lax.broadcasted_iota(jnp.int32, (width, ids.shape[1]), 0).astype(F32).astype(BF)
    return jnp.where(rel == rows, jnp.ones((), BF), jnp.zeros((), BF))


def sums_kernel(share, meta, state, ids, *outs_and_scratch):
    *outs, lhs = outs_and_scratch
    channels, sensors = state.shape
    lhs[:channels] = state[...]
    lhs[channels:] = jnp.ones((COUNT_ROWS, sensors), BF)
    position = lax.broadcasted_iota(jnp.int32, (1, sensors), 1)
    own = jnp.where(position < meta[1], ids[...], -1)
    for b, out in enumerate(outs):
        hot = one_hot(own, (meta[0] ^ b) * share, share)
        sums = lax.dot_general(lhs[...], hot, (((1,), (1,)), ((), ())), preferred_element_type=F32)
        out[:channels] = sums[:channels].astype(BF)
        counts = sums[channels:]
        high = jnp.floor(counts * (1.0 / 256.0))
        row = lax.broadcasted_iota(jnp.int32, counts.shape, 0)
        out[channels:] = jnp.where(row == 0, high, counts - 256.0 * high).astype(BF)


def split3(x):
    high = x.astype(BF)
    rest = x - high.astype(F32)
    mid = rest.astype(BF)
    return high, mid, (rest - mid.astype(F32)).astype(BF)


def pool_kernel(pieces, w_value, *refs):
    blocks, (pooled, values) = refs[:pieces], refs[pieces:]
    channels = pooled.shape[0]
    total = blocks[0][...].astype(F32)
    for ref in blocks[1:]:
        total = total + ref[...].astype(F32)
    counts = 256.0 * total[channels : channels + 1] + total[channels + 1 : channels + 2]
    mean = total[:channels] / jnp.maximum(counts, 1.0)
    pooled[...] = mean
    heads, size = w_value.shape[0], w_value.shape[1]
    for h in range(heads):
        out = jnp.zeros((size, mean.shape[1]), F32)
        for part in split3(mean[h * size : (h + 1) * size]):
            out = out + jnp.dot(w_value[h], part, preferred_element_type=F32)
        values[h * size : (h + 1) * size] = out.astype(BF)


def weights_kernel(share, source, target, weights):
    heads, _, clusters = target.shape
    for h in range(heads):
        s_hi, s_mid, s_lo = split3(source[h])
        t_hi, t_mid, t_lo = split3(target[h])
        left = jnp.concatenate([t_hi, t_hi, t_mid, t_hi, t_lo, t_mid], axis=0)
        right = jnp.concatenate([s_hi, s_mid, s_hi, s_lo, s_hi, s_mid], axis=0)
        scores = lax.dot_general(left, right, (((0,), (0,)), ((), ())), preferred_element_type=F32)
        scores = jnp.maximum(scores, 0.0)
        raised = jnp.exp(scores - jnp.max(scores, axis=0, keepdims=True))
        scale = 1.0 / jnp.sum(raised, axis=0, keepdims=True)
        weights[h] = (raised * scale).astype(BF)


def attend_kernel(values, weights, pooled, out):
    heads, _, share = weights.shape
    parts, channels, _ = values.shape
    size = channels // heads
    for h in range(heads):
        rows = slice(h * size, (h + 1) * size)
        every = jnp.concatenate([values[p, rows] for p in range(parts)], axis=1)
        attended = jnp.dot(every, weights[h], preferred_element_type=F32)
        out[rows] = (pooled[rows] + attended).astype(BF)


def fold_kernel(blocks, *refs):
    parts, (w, out) = refs[:blocks], refs[blocks:]
    coarse = jnp.concatenate([r[...] for r in parts], axis=0)
    out[...] = jnp.dot(w[...], coarse, preferred_element_type=F32).astype(BF)


def hop_kernel(blocks, tile, meta, cols, *refs):
    parts = refs[:blocks]
    left, right, adj, adj_left, adj_right, w, out, ext, one, two = refs[blocks:]
    channels, rows = parts[0].shape
    total = channels * blocks
    tiles = rows // tile
    position = lax.broadcasted_iota(jnp.int32, (1, rows), 1)
    keep = position < meta[1]
    ext[:, : 2 * tile] = left[...]
    ext[:, 2 * tile + rows :] = right[...]
    for k, part in enumerate(parts):
        ext[k * channels : (k + 1) * channels, 2 * tile : 2 * tile + rows] = jnp.where(
            keep, part[...], jnp.zeros((), BF)
        )

    def pick(ref, at):
        return jnp.concatenate(
            [ref[:, pl.ds(pl.multiple_of(a * tile, tile), tile)] for a in at], axis=1
        )

    kb = adj.shape[1]
    stack = lambda a: a.reshape(kb * tile, tile)
    first = pick(ext, [cols[tiles * kb + k] for k in range(kb)])
    one[:, :tile] = jnp.dot(first, stack(adj_left[...]), preferred_element_type=F32).astype(BF)
    last = pick(ext, [cols[tiles * kb + kb + k] + tiles + 1 for k in range(kb)])
    one[:, (tiles + 1) * tile :] = jnp.dot(
        last, stack(adj_right[...]), preferred_element_type=F32
    ).astype(BF)

    def hop(source, shift, target, t):
        picked = pick(source, [cols[t * kb + k] + shift for k in range(kb)])
        made = jnp.dot(picked, stack(adj[t]), preferred_element_type=F32)
        spot = lax.broadcasted_iota(jnp.int32, (1, tile), 1) + t * tile
        return jnp.where(spot < meta[1], made, 0.0).astype(BF)

    def step_one(t, _):
        one[:, pl.ds(pl.multiple_of((t + 1) * tile, tile), tile)] = hop(ext, 1, one, t)
        return 0

    lax.fori_loop(0, tiles, step_one, 0, unroll=2)

    def step_two(t, _):
        two[:, pl.ds(pl.multiple_of(t * tile, tile), tile)] = hop(one, 0, two, t)
        return 0

    lax.fori_loop(0, tiles, step_two, 0, unroll=2)
    width = 2 * tile

    def gates(c, _):
        at = lambda s: pl.ds(pl.multiple_of(c * width + s, tile), width)
        acc = jnp.dot(w[0], ext[:, at(2 * tile)], preferred_element_type=F32)
        acc = acc + jnp.dot(w[1], one[:, at(tile)], preferred_element_type=F32)
        acc = acc + jnp.dot(w[2], two[:, at(0)], preferred_element_type=F32)
        out[:, at(0)] = acc
        return 0

    lax.fori_loop(0, rows // width, gates, 0)


def final_kernel(places, n_given, share, tile, meta, ccols, *refs):
    given = refs[:n_given]
    ctiles, ids, partial, terms, inputs, state, out, coarse, mixed = refs[n_given:]
    outputs = coarse.shape[0]
    clusters = coarse.shape[1]
    for ref, src, dst, rows, b, absolute in places:
        owner = b if absolute else meta[0] ^ b
        at = pl.ds(pl.multiple_of(owner * share, share), share)
        coarse[dst : dst + rows, at] = given[ref][src : src + rows]
    kc = ctiles.shape[1]

    def mix(t, _):
        picked = jnp.concatenate(
            [
                coarse[:, pl.ds(pl.multiple_of(ccols[t * kc + k] * tile, tile), tile)]
                for k in range(kc)
            ],
            axis=1,
        )
        at = pl.ds(pl.multiple_of(t * tile, tile), tile)
        made = jnp.dot(picked, ctiles[t].reshape(kc * tile, tile), preferred_element_type=F32)
        mixed[:, at] = (coarse[:, at].astype(F32) + made).astype(BF)
        return 0

    lax.fori_loop(0, clusters // tile, mix, 0, unroll=2)
    sensors = state.shape[1]
    channels = state.shape[0]
    width = 2 * tile

    def step(c, _):
        at = pl.ds(pl.multiple_of(c * width, width), width)
        own = ids[:, at]
        hot = jnp.concatenate(
            [one_hot(own, f, share) for f in range(0, clusters, share)], axis=0
        )
        sums = partial[:, at] + jnp.dot(mixed[...], hot, preferred_element_type=F32)
        x = inputs[:, at].astype(F32)
        given_terms = terms[:, 2:3] + terms[:, 0:1] * x[0:1] + terms[:, 1:2] * x[1:2]
        update = jax.nn.sigmoid(given_terms[:channels] + sums[:channels])
        reset = jax.nn.sigmoid(
            given_terms[channels : 2 * channels] + sums[channels : 2 * channels]
        )
        candidate = jnp.tanh(given_terms[2 * channels :] + reset * sums[2 * channels :])
        old = state[:, at].astype(F32)
        spot = lax.broadcasted_iota(jnp.int32, (1, width), 1) + c * width
        new = update * old + (1.0 - update) * candidate
        out[:, at] = jnp.where(spot < meta[1], new, 0.0).astype(BF)
        return 0

    lax.fori_loop(0, sensors // width, step, 0)


def flip(n, b):
    return [(i, i ^ b) for i in range(n)]


def shifts(array, axis):
    n = lax.axis_size(axis)
    return [array] + [
        lax.ppermute(array, axis, [((i + k) % n, i) for i in range(n)]) for k in range(1, n)
    ]


def gather_dom(block):
    n = lax.axis_size("dom")
    rows = block.shape[0]
    send = lambda x, b: lax.ppermute(x, "dom", flip(n, b))
    if n != 8:
        every = lax.all_gather(block, "dom", axis=0, tiled=True)
        return [every], [(0, b * rows, 0, rows, b, True) for b in range(n)]
    half = rows // 2
    beside = send(block, 2)
    behind = send(block, 4)
    core = send(block, 1)
    top = send(beside[:half], 4)
    bottom = send(behind[half:], 2)
    other = send(jnp.concatenate([beside, behind, top, bottom], axis=0), 1)
    places = [
        (0, 0, 0, rows, 0, False),
        (1, 0, 0, rows, 1, False),
        (2, 0, 0, rows, 2, False),
        (3, 0, 0, rows, 4, False),
        (4, 0, 0, half, 6, False),
        (5, 0, half, half, 6, False),
        (6, 0, 0, rows, 3, False),
        (6, rows, 0, rows, 5, False),
        (6, 2 * rows, 0, rows, 7, False),
    ]
    return [block, core, beside, behind, top, bottom, other], places


def body(
    state,
    inputs,
    adj_tiles,
    adj_cols,
    valid_rows,
    cluster_of,
    w_gates,
    w_input,
    bias,
    w_value,
    source_emb,
    target_emb,
    coarse_tiles,
    coarse_cols,
):
    channels, rows = state.shape
    clusters = source_emb.shape[2]
    n_dom, n_feat = lax.axis_size("dom"), lax.axis_size("feat")
    share = clusters // n_dom
    tiles, kb, tile, _ = adj_tiles.shape
    me, feat = lax.axis_index("dom"), lax.axis_index("feat")
    meta = jnp.stack([me.astype(jnp.int32), valid_rows[0]])
    ids = cluster_of[None, :]
    total = channels * n_feat
    outputs = 3 * channels
    sds = jax.ShapeDtypeStruct

    blocks = shifts(state, "feat")

    pieces = call(
        functools.partial(sums_kernel, share),
        [sds((channels + COUNT_ROWS, share), BF)] * n_dom,
        [meta, state, ids],
        [pltpu.VMEM((channels + COUNT_ROWS, rows), BF)],
        flops=2 * channels * rows * clusters * 3,
        bytes_accessed=8 * channels * rows,
    )
    arrived = [pieces[0]] + [lax.ppermute(pieces[b], "dom", flip(n_dom, b)) for b in range(1, n_dom)]
    pooled, values = call(
        functools.partial(pool_kernel, n_dom),
        [sds((channels, share), F32), sds((channels, share), BF)],
        [w_value] + arrived,
    )
    pad = [(0, 0), (0, -source_emb.shape[1] % 16), (0, 0)]
    source = lax.dynamic_slice_in_dim(source_emb, me * share, share, 2)
    weights = call(
        functools.partial(weights_kernel, share),
        sds((source.shape[0], clusters, share), BF),
        [jnp.pad(source, pad), jnp.pad(target_emb, pad)],
        flops=source.shape[0] * clusters * share * 4000,
    )
    every_value = lax.all_gather(values, "dom", axis=0)
    own_coarse = call(attend_kernel, sds((channels, share), BF), [every_value, weights, pooled])
    coarse_blocks = shifts(own_coarse, "feat")

    w = jnp.transpose(w_gates, (2, 0, 1, 3)).reshape(4, outputs, total)
    w = lax.dynamic_slice_in_dim(jnp.concatenate([w, w], axis=2), feat * channels, total, 2)
    folded = call(
        functools.partial(fold_kernel, n_feat),
        sds((outputs, share), BF),
        coarse_blocks + [w[3]],
    )
    given, places = gather_dom(folded)

    up = [(i, (i + 1) % n_dom) for i in range(n_dom)]
    down = [(j, i) for i, j in up]
    spot = jnp.arange(rows, dtype=jnp.int32)
    keep = (spot < valid_rows[0]).astype(BF)

    def edge(t):
        made = adj_tiles[t] * keep[t * tile : (t + 1) * tile]
        offsets = (adj_cols[t] - t).astype(BF)
        offsets = jnp.broadcast_to(offsets[:, None, None], (kb, 16, tile))
        return jnp.concatenate([made, offsets], axis=1)

    from_left = lax.ppermute(edge(tiles - 1), "dom", up)
    from_right = lax.ppermute(edge(0), "dom", down)
    cols = jnp.concatenate(
        [
            adj_cols.reshape(-1),
            from_left[:, tile, 0].astype(jnp.int32),
            from_right[:, tile, 0].astype(jnp.int32),
        ]
    )
    tail = jnp.concatenate([x[:, rows - 2 * tile :] for x in blocks], axis=0)
    head = jnp.concatenate([x[:, : 2 * tile] for x in blocks], axis=0)
    left = lax.ppermute(tail * keep[rows - 2 * tile :], "dom", up)
    right = lax.ppermute(head * keep[: 2 * tile], "dom", down)
    partial = call(
        functools.partial(hop_kernel, n_feat, tile),
        sds((outputs, rows), F32),
        [meta, cols]
        + blocks
        + [left, right, adj_tiles, from_left[:, :tile], from_right[:, :tile], w[:3]],
        [
            pltpu.VMEM((total, rows + 4 * tile), BF),
            pltpu.VMEM((total, rows + 2 * tile), BF),
            pltpu.VMEM((total, rows), BF),
        ],
        flops=2 * total * rows * (4 * kb * tile + 3 * outputs),
        bytes_accessed=8 * total * rows,
    )

    terms = jnp.concatenate(
        [w_input.reshape(outputs, -1).astype(F32), bias.reshape(outputs, 1)], axis=1
    )
    return call(
        functools.partial(final_kernel, places, len(given), share, tile),
        sds((channels, rows), BF),
        [meta, coarse_cols.reshape(-1)]
        + given
        + [coarse_tiles, ids, partial, terms, inputs, state],
        [pltpu.VMEM((outputs, clusters), BF)] * 2,
        flops=2 * outputs * rows * clusters,
        bytes_accessed=8 * outputs * rows,
    )


def solution(mesh):
    return jax.shard_map(
        body,
        mesh=mesh,
        in_specs=(
            P("feat", "dom"),
            P(None, "dom"),
            P("dom", None, None, None),
            P("dom", None),
            P("dom"),
            P("dom"),
            P(None, "feat", None, None),
            P(None, "feat", None),
            P(None, "feat"),
            P("feat", None, None),
            P("feat", None, None),
            P("feat", None, None),
            P(),
            P(),
        ),
        out_specs=P("feat", "dom"),
        check_vma=False,
    )
```

```python
import functools

import jax
import jax.numpy as jnp
from jax import lax
from jax.experimental import pallas as pl
from jax.experimental.pallas import tpu as pltpu
from jax.sharding import PartitionSpec as P

BF = jnp.bfloat16
F32 = jnp.float32
VMEM = pl.BlockSpec(memory_space=pltpu.VMEM)
SMEM = pl.BlockSpec(memory_space=pltpu.SMEM)
COUNT_ROWS = 16


def call(kernel, outs, ins, scratch=(), flops=0, bytes_accessed=0, mib=16):
    specs = [SMEM if x.dtype == jnp.int32 and x.ndim == 1 else VMEM for x in ins]
    return pl.pallas_call(
        kernel,
        out_shape=outs,
        in_specs=specs,
        out_specs=jax.tree.map(lambda _: VMEM, outs),
        scratch_shapes=list(scratch),
        compiler_params=pltpu.CompilerParams(vmem_limit_bytes=mib * 2**20),
        cost_estimate=pl.CostEstimate(
            flops=int(flops), bytes_accessed=int(bytes_accessed), transcendentals=0
        ),
    )(*ins)


def one_hot(ids, first, width):
    rel = jnp.clip(ids - first, -1, width).astype(F32).astype(BF)
    rows = lax.broadcasted_iota(jnp.int32, (width, ids.shape[1]), 0).astype(F32).astype(BF)
    return jnp.where(rel == rows, jnp.ones((), BF), jnp.zeros((), BF))


def split_counts(rows, counts):
    high = jnp.floor(counts * (1.0 / 256.0))
    row = lax.broadcasted_iota(jnp.int32, (rows, counts.shape[1]), 0)
    return jnp.where(row == 0, high, counts - 256.0 * high).astype(BF)


def join_counts(rows):
    return 256.0 * rows[0:1] + rows[1:2]


def sums_kernel(share, meta, state, ids, kept, sent, lhs):
    channels, sensors = state.shape
    lhs[:channels] = state[...]
    lhs[channels:] = jnp.ones((COUNT_ROWS, sensors), BF)
    position = lax.broadcasted_iota(jnp.int32, (1, sensors), 1)
    own = jnp.where(position < meta[1], ids[...], -1)
    for e in range(kept.shape[0]):
        for other in (1, 0):
            hot = one_hot(own, (meta[0] ^ (2 * e + other)) * share, share)
            sums = lax.dot_general(
                lhs[...], hot, (((1,), (1,)), ((), ())), preferred_element_type=F32
            )
            if other:
                sent[e, :channels] = sums[:channels].astype(BF)
                sent[e, channels:] = split_counts(COUNT_ROWS, sums[channels:])
            else:
                kept[e] = sums


def pair_kernel(kept, arrived, own, *outs):
    channels = own.shape[0] - COUNT_ROWS
    for e, out in enumerate((own,) + outs):
        came = arrived[e].astype(F32)
        sums = kept[e, :channels] + came[:channels]
        counts = kept[e, channels:] + join_counts(came[channels:])
        out[:channels] = sums.astype(out.dtype)
        out[channels:] = split_counts(COUNT_ROWS, counts).astype(out.dtype)


def split3(x):
    high = x.astype(BF)
    rest = x - high.astype(F32)
    mid = rest.astype(BF)
    return high, mid, (rest - mid.astype(F32)).astype(BF)


def pool_kernel(pieces, w_value, *refs):
    blocks, (pooled, values) = refs[:pieces], refs[pieces:]
    channels = pooled.shape[0]
    total = blocks[0][...].astype(F32)
    for ref in blocks[1:]:
        total = total + ref[...].astype(F32)
    counts = join_counts(total[channels:])
    mean = total[:channels] / jnp.maximum(counts, 1.0)
    pooled[...] = mean
    heads, size = w_value.shape[0], w_value.shape[1]
    for h in range(heads):
        out = jnp.zeros((size, mean.shape[1]), F32)
        for part in split3(mean[h * size : (h + 1) * size]):
            out = out + jnp.dot(w_value[h], part, preferred_element_type=F32)
        values[h * size : (h + 1) * size] = out.astype(BF)


def weights_kernel(share, source, target, weights):
    heads, _, clusters = target.shape
    for h in range(heads):
        s_hi, s_mid, s_lo = split3(source[h])
        t_hi, t_mid, t_lo = split3(target[h])
        left = jnp.concatenate([t_hi, t_hi, t_mid, t_hi, t_lo, t_mid], axis=0)
        right = jnp.concatenate([s_hi, s_mid, s_hi, s_lo, s_hi, s_mid], axis=0)
        scores = lax.dot_general(left, right, (((0,), (0,)), ((), ())), preferred_element_type=F32)
        scores = jnp.maximum(scores, 0.0)
        raised = jnp.exp(scores - jnp.max(scores, axis=0, keepdims=True))
        scale = 1.0 / jnp.sum(raised, axis=0, keepdims=True)
        weights[h] = (raised * scale).astype(BF)


def attend_kernel(values, weights, pooled, out):
    heads, _, share = weights.shape
    parts, channels, _ = values.shape
    size = channels // heads
    for h in range(heads):
        rows = slice(h * size, (h + 1) * size)
        every = jnp.concatenate([values[p, rows] for p in range(parts)], axis=1)
        attended = jnp.dot(every, weights[h], preferred_element_type=F32)
        out[rows] = (pooled[rows] + attended).astype(BF)


def fold_kernel(blocks, meta, *refs):
    parts, (w, out, coarse) = refs[:blocks], refs[blocks:]
    channels = parts[0].shape[0]
    for k, part in enumerate(parts):
        coarse[pl.ds(pl.multiple_of((meta[2] ^ k) * channels, channels), channels)] = part[...]
    out[...] = jnp.dot(w[...], coarse[...], preferred_element_type=F32).astype(BF)


def band_kernel(meta, cols, adj, band, edge_last, edge_first, total):
    tiles, kb, tile, _ = adj.shape

    def step(t, _):
        spot = lax.broadcasted_iota(jnp.int32, (1, tile), 1) + t * tile
        total[: 2 * tile] = jnp.zeros((2 * tile, tile), F32)
        total[2 * tile :] = adj[t, kb - 1].astype(F32)
        for k in range(kb - 1):
            at = pl.ds(pl.multiple_of((cols[t * kb + k] - t) * tile, tile), tile)
            total[at] = total[at] + adj[t, k].astype(F32)
        band[t] = jnp.where(spot < meta[1], total[...], 0.0).astype(BF)
        return 0

    lax.fori_loop(0, tiles, step, 0)
    half = 3 * tile // 2
    for edge, t in ((edge_last, tiles - 1), (edge_first, 0)):
        edge[:, :tile] = band[t, :half]
        edge[:, tile:] = band[t, half:]


def pair_weights(tile, a, b):
    none = jnp.zeros((tile, tile), BF)
    return jnp.concatenate(
        [jnp.concatenate([a, none], axis=0), jnp.concatenate([none, b], axis=0)], axis=1
    )


def hop_one_kernel(blocks, tile, meta, *refs):
    parts = refs[:blocks]
    left, right, band, ext, one = refs[blocks:]
    channels, rows = parts[0].shape
    total = ext.shape[0]
    n = total // channels
    tiles = rows // tile
    half = 3 * tile // 2
    keep = lax.broadcasted_iota(jnp.int32, (1, rows), 1) < meta[1]
    ends = slice(0, 2 * tile), slice(2 * tile + rows, 4 * tile + rows)
    for k in range(n):
        at = pl.ds(pl.multiple_of((meta[2] ^ k) * channels, channels), channels)
        part = parts[k][...]
        if k == 3 and blocks > n:
            part = jnp.where((meta[2] + 1) % 4 < 2, parts[4][...], part)
        ext[at, 2 * tile : 2 * tile + rows] = jnp.where(keep, part, jnp.zeros((), BF))
        for end, beside in zip(ends, (left, right)):
            ext[at, end] = beside[k * channels : (k + 1) * channels]

    def edge(ref):
        return jnp.concatenate(
            [ref[total : total + half, :tile], ref[total : total + half, tile:]], axis=0
        )

    def hop(u, a, b):
        at = lambda width: pl.ds(pl.multiple_of(2 * u * tile, 2 * tile), width)
        made = jnp.dot(ext[:, at(4 * tile)], pair_weights(tile, a, b), preferred_element_type=F32)
        one[:, at(2 * tile)] = made.astype(BF)

    hop(0, edge(left), band[0])
    hop(tiles // 2, band[tiles - 1], edge(right))

    def step(u, _):
        hop(u, band[2 * u - 1], band[2 * u])
        return 0

    lax.fori_loop(1, tiles // 2, step, 0, unroll=True)


def hop_two_kernel(tile, ext, one, band, w, out):
    def step(u, _):
        at = lambda s, width: pl.ds(pl.multiple_of(2 * u * tile + s, tile), width)
        weights = pair_weights(tile, band[2 * u], band[2 * u + 1])
        two = jnp.dot(one[:, at(0, 4 * tile)], weights, preferred_element_type=F32).astype(BF)
        acc = jnp.dot(w[0], ext[:, at(2 * tile, 2 * tile)], preferred_element_type=F32)
        acc = acc + jnp.dot(w[1], one[:, at(tile, 2 * tile)], preferred_element_type=F32)
        acc = acc + jnp.dot(w[2], two, preferred_element_type=F32)
        out[:, at(0, 2 * tile)] = acc
        return 0

    lax.fori_loop(0, out.shape[1] // (2 * tile), step, 0, unroll=2)


def final_kernel(places, n_given, share, tile, meta, ccols, *refs):
    given = refs[:n_given]
    ctiles, ids, partial, terms, inputs, state, out, coarse, mixed = refs[n_given:]
    outputs = coarse.shape[0]
    clusters = coarse.shape[1]
    for ref, src, dst, rows, b, absolute in places:
        owner = b if absolute else meta[0] ^ b
        at = pl.ds(pl.multiple_of(owner * share, share), share)
        coarse[dst : dst + rows, at] = given[ref][src : src + rows]
    kc = ctiles.shape[1]

    def mix(t, _):
        picked = jnp.concatenate(
            [
                coarse[:, pl.ds(pl.multiple_of(ccols[t * kc + k] * tile, tile), tile)]
                for k in range(kc)
            ],
            axis=1,
        )
        at = pl.ds(pl.multiple_of(t * tile, tile), tile)
        made = jnp.dot(picked, ctiles[t].reshape(kc * tile, tile), preferred_element_type=F32)
        mixed[:, at] = (coarse[:, at].astype(F32) + made).astype(BF)
        return 0

    lax.fori_loop(0, clusters // tile, mix, 0, unroll=2)
    sensors = state.shape[1]
    channels = state.shape[0]
    width = 2 * tile

    def step(c, _):
        at = pl.ds(pl.multiple_of(c * width, width), width)
        own = ids[:, at]
        hot = jnp.concatenate(
            [one_hot(own, f, share) for f in range(0, clusters, share)], axis=0
        )
        sums = partial[:, at] + jnp.dot(mixed[...], hot, preferred_element_type=F32)
        x = inputs[:, at].astype(F32)
        given_terms = terms[:, 2:3] + terms[:, 0:1] * x[0:1] + terms[:, 1:2] * x[1:2]
        update = jax.nn.sigmoid(given_terms[:channels] + sums[:channels])
        reset = jax.nn.sigmoid(
            given_terms[channels : 2 * channels] + sums[channels : 2 * channels]
        )
        candidate = jnp.tanh(given_terms[2 * channels :] + reset * sums[2 * channels :])
        old = state[:, at].astype(F32)
        spot = lax.broadcasted_iota(jnp.int32, (1, width), 1) + c * width
        new = update * old + (1.0 - update) * candidate
        out[:, at] = jnp.where(spot < meta[1], new, 0.0).astype(BF)
        return 0

    lax.fori_loop(0, sensors // width, step, 0)


def flip(n, b):
    return [(i, i ^ b) for i in range(n)]


def swap(array, axis, b):
    return lax.ppermute(array, axis, flip(lax.axis_size(axis), b))


def exchange(array):
    n = lax.axis_size("feat")
    if n != 4:
        return [array] + [swap(array, "feat", k) for k in range(1, n)]
    far = swap(array, "feat", 2)
    near = swap(array, "feat", 1)
    inner = lax.ppermute(array, "feat", [(1, 2), (2, 1)])
    return [array, near, far, inner]


def gather_dom(block):
    n = lax.axis_size("dom")
    rows = block.shape[0]
    send = lambda x, b: lax.ppermute(x, "dom", flip(n, b))
    if n != 8:
        every = lax.all_gather(block, "dom", axis=0, tiled=True)
        return [every], [(0, b * rows, 0, rows, b, True) for b in range(n)]
    half = rows // 2
    beside = send(block, 2)
    behind = send(block, 4)
    core = send(block, 1)
    top = send(beside[:half], 4)
    bottom = send(behind[half:], 2)
    other = send(jnp.concatenate([beside, behind, top, bottom], axis=0), 1)
    places = [
        (0, 0, 0, rows, 0, False),
        (1, 0, 0, rows, 1, False),
        (2, 0, 0, rows, 2, False),
        (3, 0, 0, rows, 4, False),
        (4, 0, 0, half, 6, False),
        (5, 0, half, half, 6, False),
        (6, 0, 0, rows, 3, False),
        (6, rows, 0, rows, 5, False),
        (6, 2 * rows, 0, rows, 7, False),
    ]
    return [block, core, beside, behind, top, bottom, other], places


def body(
    state,
    inputs,
    adj_tiles,
    adj_cols,
    valid_rows,
    cluster_of,
    w_gates,
    w_input,
    bias,
    w_value,
    source_emb,
    target_emb,
    coarse_tiles,
    coarse_cols,
):
    channels, rows = state.shape
    clusters = source_emb.shape[2]
    n_dom, n_feat = lax.axis_size("dom"), lax.axis_size("feat")
    share = clusters // n_dom
    tiles, kb, tile, _ = adj_tiles.shape
    me, feat = lax.axis_index("dom"), lax.axis_index("feat")
    meta = jnp.stack([me.astype(jnp.int32), valid_rows[0], feat.astype(jnp.int32)])
    ids = cluster_of[None, :]
    total = channels * n_feat
    outputs = 3 * channels
    sds = jax.ShapeDtypeStruct

    kept, sent = call(
        functools.partial(sums_kernel, share),
        [
            sds((n_dom // 2, channels + COUNT_ROWS, share), F32),
            sds((n_dom // 2, channels + COUNT_ROWS, share), BF),
        ],
        [meta, state, ids],
        [pltpu.VMEM((channels + COUNT_ROWS, rows), BF)],
        flops=2 * channels * rows * clusters * 3,
        bytes_accessed=8 * channels * rows,
    )
    sent, state_late = lax.optimization_barrier((sent, state))
    blocks = exchange(state_late)
    pieces = call(
        pair_kernel,
        [sds((channels + COUNT_ROWS, share), F32)]
        + [sds((channels + COUNT_ROWS, share), BF)] * (n_dom // 2 - 1),
        [kept, lax.ppermute(sent, "dom", flip(n_dom, 1))],
    )
    pieces, source_emb, target_emb, w_gates, adj_tiles, w_input, coarse_cols = (
        lax.optimization_barrier(
            (pieces, source_emb, target_emb, w_gates, adj_tiles, w_input, coarse_cols)
        )
    )
    arrived = [pieces[0]] + [
        lax.ppermute(pieces[e], "dom", flip(n_dom, 2 * e)) for e in range(1, n_dom // 2)
    ]
    pad = [(0, 0), (0, -source_emb.shape[1] % 16), (0, 0)]
    source = lax.dynamic_slice_in_dim(source_emb, me * share, share, 2)
    weights = call(
        functools.partial(weights_kernel, share),
        sds((source.shape[0], clusters, share), BF),
        [jnp.pad(source, pad), jnp.pad(target_emb, pad)],
        flops=source.shape[0] * clusters * share * 4000,
    )
    w = jnp.transpose(w_gates, (2, 0, 1, 3)).reshape(4, outputs, total)
    w_own, w_coarse = w[:3], w[3]
    band, edge_last, edge_first = call(
        band_kernel,
        [sds((tiles, 3 * tile, tile), BF)] + [sds((3 * tile // 2, 2 * tile), BF)] * 2,
        [meta, adj_cols.reshape(-1), adj_tiles],
        [pltpu.VMEM((3 * tile, tile), F32)],
        flops=10**9,
    )
    terms = jnp.concatenate(
        [w_input.reshape(outputs, -1).astype(F32), bias.reshape(outputs, 1)], axis=1
    )
    coarse_at = coarse_cols.reshape(-1)
    ready = (weights, w_own, w_coarse, band, edge_last, edge_first, terms, coarse_at)
    arrived, ready = lax.optimization_barrier((arrived, ready))
    weights, w_own, w_coarse, band, edge_last, edge_first, terms, coarse_at = ready
    pooled, values = call(
        functools.partial(pool_kernel, n_dom // 2),
        [sds((channels, share), F32), sds((channels, share), BF)],
        [w_value] + arrived,
    )
    every_value = lax.all_gather(values, "dom", axis=0)
    if n_feat == 4:
        every_value, blocks[2] = lax.optimization_barrier((every_value, blocks[2]))
        blocks.append(lax.ppermute(blocks[2], "feat", [(1, 0), (2, 3)]))
    own_coarse = call(attend_kernel, sds((channels, share), BF), [every_value, weights, pooled])
    coarse_blocks = [own_coarse] + [swap(own_coarse, "feat", k) for k in range(1, n_feat)]
    coarse_blocks, blocks = lax.optimization_barrier((coarse_blocks, blocks))
    folded = call(
        functools.partial(fold_kernel, n_feat),
        sds((outputs, share), BF),
        [meta] + coarse_blocks + [w_coarse],
        [pltpu.VMEM((total, share), BF)],
    )
    given, places = gather_dom(folded)

    up = [(i, (i + 1) % n_dom) for i in range(n_dom)]
    down = [(j, i) for i, j in up]
    keep = (jnp.arange(rows, dtype=jnp.int32) < valid_rows[0]).astype(BF)

    def edge_of(lanes, weights):
        ends = [x[:, lanes] for x in blocks]
        if n_feat == 4:
            ends[3:] = [jnp.where((feat == 0) | (feat == 3), ends[4], ends[3])]
        return jnp.concatenate([x * keep[lanes] for x in ends] + [weights], axis=0)

    left = lax.ppermute(edge_of(slice(rows - 2 * tile, rows), edge_last), "dom", up)
    right = lax.ppermute(edge_of(slice(0, 2 * tile), edge_first), "dom", down)
    ext, one = call(
        functools.partial(hop_one_kernel, len(blocks), tile),
        [sds((total, rows + 4 * tile), BF), sds((total, rows + 2 * tile), BF)],
        [meta] + blocks + [left, right, band],
        flops=2 * total * rows * kb * tile,
        bytes_accessed=8 * total * rows,
    )
    partial = call(
        functools.partial(hop_two_kernel, tile),
        sds((outputs, rows), F32),
        [ext, one, band, w_own],
        flops=2 * total * rows * (kb * tile + 3 * outputs),
        bytes_accessed=8 * total * rows,
    )

    return call(
        functools.partial(final_kernel, places, len(given), share, tile),
        sds((channels, rows), BF),
        [meta, coarse_at]
        + given
        + [coarse_tiles, ids, partial, terms, inputs, state],
        [pltpu.VMEM((outputs, clusters), BF)] * 2,
        flops=2 * outputs * rows * clusters,
        bytes_accessed=8 * outputs * rows,
    )


def solution(mesh):
    return jax.shard_map(
        body,
        mesh=mesh,
        in_specs=(
            P("feat", "dom"),
            P(None, "dom"),
            P("dom", None, None, None),
            P("dom", None),
            P("dom"),
            P("dom"),
            P(None, "feat", None, None),
            P(None, "feat", None),
            P(None, "feat"),
            P("feat", None, None),
            P("feat", None, None),
            P("feat", None, None),
            P(),
            P(),
        ),
        out_specs=P("feat", "dom"),
        check_vma=False,
    )
```

```python
import functools

import jax
import jax.numpy as jnp
from jax import lax
from jax.experimental import pallas as pl
from jax.experimental.pallas import tpu as pltpu
from jax.sharding import PartitionSpec as P

BF = jnp.bfloat16
F32 = jnp.float32
VMEM = pl.BlockSpec(memory_space=pltpu.VMEM)
SMEM = pl.BlockSpec(memory_space=pltpu.SMEM)
COUNT_ROWS = 16


def call(kernel, outs, ins, scratch=(), flops=0, bytes_accessed=0, mib=16):
    specs = [SMEM if x.dtype == jnp.int32 and x.ndim == 1 else VMEM for x in ins]
    return pl.pallas_call(
        kernel,
        out_shape=outs,
        in_specs=specs,
        out_specs=jax.tree.map(lambda _: VMEM, outs),
        scratch_shapes=list(scratch),
        compiler_params=pltpu.CompilerParams(vmem_limit_bytes=mib * 2**20),
        cost_estimate=pl.CostEstimate(
            flops=int(flops), bytes_accessed=int(bytes_accessed), transcendentals=0
        ),
    )(*ins)


def one_hot(ids, first, width):
    rel = jnp.clip(ids - first, -1, width).astype(F32).astype(BF)
    rows = lax.broadcasted_iota(jnp.int32, (width, ids.shape[1]), 0).astype(F32).astype(BF)
    return jnp.where(rel == rows, jnp.ones((), BF), jnp.zeros((), BF))


def split_counts(rows, counts):
    high = jnp.floor(counts * (1.0 / 256.0))
    row = lax.broadcasted_iota(jnp.int32, (rows, counts.shape[1]), 0)
    return jnp.where(row == 0, high, counts - 256.0 * high).astype(BF)


def join_counts(rows):
    return 256.0 * rows[0:1] + rows[1:2]


def sums_kernel(share, meta, state, ids, kept, sent, lhs):
    channels, sensors = state.shape
    lhs[:channels] = state[...]
    lhs[channels:] = jnp.ones((COUNT_ROWS, sensors), BF)
    position = lax.broadcasted_iota(jnp.int32, (1, sensors), 1)
    own = jnp.where(position < meta[1], ids[...], -1)
    for e in range(kept.shape[0]):
        for other in (1, 0):
            hot = one_hot(own, (meta[0] ^ (2 * e + other)) * share, share)
            sums = lax.dot_general(
                lhs[...], hot, (((1,), (1,)), ((), ())), preferred_element_type=F32
            )
            if other:
                sent[e, :channels] = sums[:channels].astype(BF)
                sent[e, channels:] = split_counts(COUNT_ROWS, sums[channels:])
            else:
                kept[e] = sums


def pair_kernel(kept, arrived, own, *outs):
    channels = own.shape[0] - COUNT_ROWS
    for e, out in enumerate((own,) + outs):
        came = arrived[e].astype(F32)
        sums = kept[e, :channels] + came[:channels]
        counts = kept[e, channels:] + join_counts(came[channels:])
        out[:channels] = sums.astype(out.dtype)
        out[channels:] = split_counts(COUNT_ROWS, counts).astype(out.dtype)


def split3(x):
    high = x.astype(BF)
    rest = x - high.astype(F32)
    mid = rest.astype(BF)
    return high, mid, (rest - mid.astype(F32)).astype(BF)


def pool_kernel(pieces, w_value, *refs):
    blocks, (pooled, values) = refs[:pieces], refs[pieces:]
    channels = pooled.shape[0]
    total = blocks[0][...].astype(F32)
    for ref in blocks[1:]:
        total = total + ref[...].astype(F32)
    counts = join_counts(total[channels:])
    mean = total[:channels] / jnp.maximum(counts, 1.0)
    pooled[...] = mean
    heads, size = w_value.shape[0], w_value.shape[1]
    for h in range(heads):
        out = jnp.zeros((size, mean.shape[1]), F32)
        for part in split3(mean[h * size : (h + 1) * size]):
            out = out + jnp.dot(w_value[h], part, preferred_element_type=F32)
        values[h * size : (h + 1) * size] = out.astype(BF)


def weights_kernel(share, source, target, weights):
    heads, _, clusters = target.shape
    for h in range(heads):
        s_hi, s_mid, s_lo = split3(source[h])
        t_hi, t_mid, t_lo = split3(target[h])
        left = jnp.concatenate([t_hi, t_hi, t_mid, t_hi, t_lo, t_mid], axis=0)
        right = jnp.concatenate([s_hi, s_mid, s_hi, s_lo, s_hi, s_mid], axis=0)
        scores = lax.dot_general(left, right, (((0,), (0,)), ((), ())), preferred_element_type=F32)
        scores = jnp.maximum(scores, 0.0)
        raised = jnp.exp(scores - jnp.max(scores, axis=0, keepdims=True))
        scale = 1.0 / jnp.sum(raised, axis=0, keepdims=True)
        weights[h] = (raised * scale).astype(BF)


def attend_kernel(values, weights, pooled, out):
    heads, _, share = weights.shape
    parts, channels, _ = values.shape
    size = channels // heads
    for h in range(heads):
        rows = slice(h * size, (h + 1) * size)
        every = jnp.concatenate([values[p, rows] for p in range(parts)], axis=1)
        attended = jnp.dot(every, weights[h], preferred_element_type=F32)
        out[rows] = (pooled[rows] + attended).astype(BF)


def fold_kernel(blocks, meta, *refs):
    parts, (w, out, coarse) = refs[:blocks], refs[blocks:]
    channels = parts[0].shape[0]
    for k, part in enumerate(parts):
        coarse[pl.ds(pl.multiple_of((meta[2] ^ k) * channels, channels), channels)] = part[...]
    out[...] = jnp.dot(w[...], coarse[...], preferred_element_type=F32).astype(BF)


def band_kernel(meta, cols, adj, terms, band, edge_last, edge_first, terms_out, total):
    tiles, kb, tile, _ = adj.shape
    terms_out[...] = terms[...]

    def step(t, _):
        spot = lax.broadcasted_iota(jnp.int32, (1, tile), 1) + t * tile
        total[: 2 * tile] = jnp.zeros((2 * tile, tile), F32)
        total[2 * tile :] = adj[t, kb - 1].astype(F32)
        for k in range(kb - 1):
            at = pl.ds(pl.multiple_of((cols[t * kb + k] - t) * tile, tile), tile)
            total[at] = total[at] + adj[t, k].astype(F32)
        band[t] = jnp.where(spot < meta[1], total[...], 0.0).astype(BF)
        return 0

    lax.fori_loop(0, tiles, step, 0)
    half = 3 * tile // 2
    for edge, t in ((edge_last, tiles - 1), (edge_first, 0)):
        edge[:, :tile] = band[t, :half]
        edge[:, tile:] = band[t, half:]


def pair_weights(tile, a, b):
    none = jnp.zeros((tile, tile), BF)
    return jnp.concatenate(
        [jnp.concatenate([a, none], axis=0), jnp.concatenate([none, b], axis=0)], axis=1
    )


def is_end(feat):
    return (feat + 1) % 4 < 2


def edge_kernel(n, tile, meta, *refs):
    *parts, edge_last, edge_first, last, first = refs
    channels, rows = parts[0].shape
    position = lax.broadcasted_iota(jnp.int32, (1, 2 * tile), 1)
    ends = (last, rows - 2 * tile, edge_last), (first, 0, edge_first)
    for out, start, weights in ends:
        keep = position + start < meta[1]
        for k in range(n):
            part = parts[k][:, start : start + 2 * tile]
            if k == 3 and len(parts) > n:
                other = parts[4][:, start : start + 2 * tile]
                part = jnp.where(is_end(meta[2]), other, part)
            out[k * channels : (k + 1) * channels] = jnp.where(keep, part, jnp.zeros((), BF))
        out[n * channels :] = weights[...]


def hop_one_kernel(n, tile, meta, *refs):
    *parts, left, right, band, ext, one = refs
    channels, rows = parts[0].shape
    total = ext.shape[0]
    tiles = rows // tile
    half = 3 * tile // 2
    keep = lax.broadcasted_iota(jnp.int32, (1, rows), 1) < meta[1]
    ends = slice(0, 2 * tile), slice(2 * tile + rows, 4 * tile + rows)
    for k in range(n):
        at = pl.ds(pl.multiple_of((meta[2] ^ k) * channels, channels), channels)
        part = parts[k][...]
        if k == 3 and len(parts) > n:
            part = jnp.where(is_end(meta[2]), parts[4][...], part)
        ext[at, 2 * tile : 2 * tile + rows] = jnp.where(keep, part, jnp.zeros((), BF))
        for end, beside in zip(ends, (left, right)):
            ext[at, end] = beside[k * channels : (k + 1) * channels]

    def edge(ref):
        return jnp.concatenate(
            [ref[total : total + half, :tile], ref[total : total + half, tile:]], axis=0
        )

    def hop(u, a, b):
        at = lambda width: pl.ds(pl.multiple_of(2 * u * tile, 2 * tile), width)
        made = jnp.dot(ext[:, at(4 * tile)], pair_weights(tile, a, b), preferred_element_type=F32)
        one[:, at(2 * tile)] = made.astype(BF)

    hop(0, edge(left), band[0])
    hop(tiles // 2, band[tiles - 1], edge(right))

    def step(u, _):
        hop(u, band[2 * u - 1], band[2 * u])
        return 0

    lax.fori_loop(1, tiles // 2, step, 0, unroll=True)


def hop_two_kernel(tile, ext, one, band, w, out):
    def step(u, _):
        at = lambda s, width: pl.ds(pl.multiple_of(2 * u * tile + s, tile), width)
        weights = pair_weights(tile, band[2 * u], band[2 * u + 1])
        two = jnp.dot(one[:, at(0, 4 * tile)], weights, preferred_element_type=F32).astype(BF)
        acc = jnp.dot(w[0], ext[:, at(2 * tile, 2 * tile)], preferred_element_type=F32)
        acc = acc + jnp.dot(w[1], one[:, at(tile, 2 * tile)], preferred_element_type=F32)
        acc = acc + jnp.dot(w[2], two, preferred_element_type=F32)
        out[:, at(0, 2 * tile)] = acc
        return 0

    lax.fori_loop(0, out.shape[1] // (2 * tile), step, 0, unroll=True)


def final_kernel(places, n_given, share, tile, meta, ccols, *refs):
    given = refs[:n_given]
    ctiles, ids, partial, terms, inputs, state, out, coarse, mixed = refs[n_given:]
    outputs = coarse.shape[0]
    clusters = coarse.shape[1]
    for ref, src, dst, rows, b, absolute in places:
        owner = b if absolute else meta[0] ^ b
        at = pl.ds(pl.multiple_of(owner * share, share), share)
        coarse[dst : dst + rows, at] = given[ref][src : src + rows]
    kc = ctiles.shape[1]

    def mix(t, _):
        picked = jnp.concatenate(
            [
                coarse[:, pl.ds(pl.multiple_of(ccols[t * kc + k] * tile, tile), tile)]
                for k in range(kc)
            ],
            axis=1,
        )
        at = pl.ds(pl.multiple_of(t * tile, tile), tile)
        made = jnp.dot(picked, ctiles[t].reshape(kc * tile, tile), preferred_element_type=F32)
        mixed[:, at] = (coarse[:, at].astype(F32) + made).astype(BF)
        return 0

    lax.fori_loop(0, clusters // tile, mix, 0, unroll=True)
    sensors = state.shape[1]
    channels = state.shape[0]
    width = 4 * tile

    def step(c, _):
        at = pl.ds(pl.multiple_of(c * width, width), width)
        own = ids[:, at]
        hot = jnp.concatenate(
            [one_hot(own, f, share) for f in range(0, clusters, share)], axis=0
        )
        sums = partial[:, at] + jnp.dot(mixed[...], hot, preferred_element_type=F32)
        x = inputs[:, at].astype(F32)
        given_terms = terms[:, 2:3] + terms[:, 0:1] * x[0:1] + terms[:, 1:2] * x[1:2]
        update = jax.nn.sigmoid(given_terms[:channels] + sums[:channels])
        reset = jax.nn.sigmoid(
            given_terms[channels : 2 * channels] + sums[channels : 2 * channels]
        )
        candidate = jnp.tanh(given_terms[2 * channels :] + reset * sums[2 * channels :])
        old = state[:, at].astype(F32)
        spot = lax.broadcasted_iota(jnp.int32, (1, width), 1) + c * width
        new = update * old + (1.0 - update) * candidate
        out[:, at] = jnp.where(spot < meta[1], new, 0.0).astype(BF)
        return 0

    lax.fori_loop(0, sensors // width, step, 0, unroll=True)


def flip(n, b):
    return [(i, i ^ b) for i in range(n)]


def swap(array, axis, b):
    return lax.ppermute(array, axis, flip(lax.axis_size(axis), b))


def gather_dom(block, *ready):
    n = lax.axis_size("dom")
    rows = block.shape[0]
    send = lambda x, b: swap(x, "dom", b)
    if n != 8:
        every = lax.all_gather(block, "dom", axis=0, tiled=True)
        return [every], [(0, b * rows, 0, rows, b, True) for b in range(n)], *ready
    half = rows // 2
    beside = send(block, 2)
    behind = send(block, 4)
    core = send(block, 1)
    (beside, behind), ready = lax.optimization_barrier(((beside, behind), ready))
    top = send(beside[:half], 4)
    bottom = send(behind[half:], 2)
    other = send(jnp.concatenate([beside, behind, top, bottom], axis=0), 1)
    places = [
        (0, 0, 0, rows, 0, False),
        (1, 0, 0, rows, 1, False),
        (2, 0, 0, rows, 2, False),
        (3, 0, 0, rows, 4, False),
        (4, 0, 0, half, 6, False),
        (5, 0, half, half, 6, False),
        (6, 0, 0, rows, 3, False),
        (6, rows, 0, rows, 5, False),
        (6, 2 * rows, 0, rows, 7, False),
    ]
    return [block, core, beside, behind, top, bottom, other], places, *ready


def body(
    state,
    inputs,
    adj_tiles,
    adj_cols,
    valid_rows,
    cluster_of,
    w_gates,
    w_input,
    bias,
    w_value,
    source_emb,
    target_emb,
    coarse_tiles,
    coarse_cols,
):
    channels, rows = state.shape
    clusters = source_emb.shape[2]
    n_dom, n_feat = lax.axis_size("dom"), lax.axis_size("feat")
    share = clusters // n_dom
    tiles, kb, tile, _ = adj_tiles.shape
    me, feat = lax.axis_index("dom"), lax.axis_index("feat")
    meta = jnp.stack([me.astype(jnp.int32), valid_rows[0], feat.astype(jnp.int32)])
    ids = cluster_of[None, :]
    total = channels * n_feat
    outputs = 3 * channels
    sds = jax.ShapeDtypeStruct

    kept, sent = call(
        functools.partial(sums_kernel, share),
        [
            sds((n_dom // 2, channels + COUNT_ROWS, share), F32),
            sds((n_dom // 2, channels + COUNT_ROWS, share), BF),
        ],
        [meta, state, ids],
        [pltpu.VMEM((channels + COUNT_ROWS, rows), BF)],
        flops=2 * channels * rows * clusters * 3,
        bytes_accessed=8 * channels * rows,
    )
    line = n_feat == 4
    sent, state_far = lax.optimization_barrier((sent, state))
    far = [swap(state_far, "feat", k) for k in range(2, n_feat) if k == 2 or not line]
    pieces = call(
        pair_kernel,
        [sds((channels + COUNT_ROWS, share), F32)]
        + [sds((channels + COUNT_ROWS, share), BF)] * (n_dom // 2 - 1),
        [kept, swap(sent, "dom", 1)],
    )
    pieces, state_near, source_emb, target_emb = lax.optimization_barrier(
        (pieces, state, source_emb, target_emb)
    )
    arrived = [pieces[0]] + [swap(pieces[e], "dom", 2 * e) for e in range(1, n_dom // 2)]
    blocks = [state, swap(state_near, "feat", 1)] + far
    pad = [(0, 0), (0, -source_emb.shape[1] % 16), (0, 0)]
    source = lax.dynamic_slice_in_dim(source_emb, me * share, share, 2)
    weights = call(
        functools.partial(weights_kernel, share),
        sds((source.shape[0], clusters, share), BF),
        [jnp.pad(source, pad), jnp.pad(target_emb, pad)],
        flops=source.shape[0] * clusters * share * 4000,
    )
    arrived, weights = lax.optimization_barrier((arrived, weights))
    pooled, values = call(
        functools.partial(pool_kernel, n_dom // 2),
        [sds((channels, share), F32), sds((channels, share), BF)],
        [w_value] + arrived,
    )
    every_value = lax.all_gather(values, "dom", axis=0)
    own_coarse = call(attend_kernel, sds((channels, share), BF), [every_value, weights, pooled])

    own_coarse, w_gates, adj_tiles, w_input, coarse_cols = lax.optimization_barrier(
        (own_coarse, w_gates, adj_tiles, w_input, coarse_cols)
    )
    coarse_blocks = [own_coarse] + [swap(own_coarse, "feat", k) for k in range(1, n_feat)]
    if line:
        own_coarse, blocks[1:3], state_inner = lax.optimization_barrier(
            (own_coarse, blocks[1:3], state)
        )
        outer = lax.ppermute(blocks[2], "feat", [(1, 0), (2, 3)])
        blocks += [lax.ppermute(state_inner, "feat", [(1, 2), (2, 1)]), outer]
    w = jnp.transpose(w_gates, (2, 0, 1, 3)).reshape(4, outputs, total)
    w_own, w_coarse = w[:3], w[3]
    edge_shape = sds((3 * tile // 2, 2 * tile), BF)
    terms = jnp.concatenate(
        [w_input.reshape(outputs, -1).astype(F32), bias.reshape(outputs, 1)], axis=1
    )
    band, edge_last, edge_first, terms = call(
        band_kernel,
        [sds((tiles, 3 * tile, tile), BF), edge_shape, edge_shape, sds(terms.shape, F32)],
        [meta, adj_cols.reshape(-1), adj_tiles, terms],
        [pltpu.VMEM((3 * tile, tile), F32)],
        flops=10**9,
    )
    coarse_at = coarse_cols.reshape(-1)
    ready = (w_own, w_coarse, band, terms, coarse_at)
    coarse_blocks, ready = lax.optimization_barrier((coarse_blocks, ready))
    w_own, w_coarse, band, terms, coarse_at = ready
    message = sds((total + 3 * tile // 2, 2 * tile), BF)
    last, first = call(
        functools.partial(edge_kernel, n_feat, tile),
        [message, message],
        [meta] + blocks + [edge_last, edge_first],
    )
    folded = call(
        functools.partial(fold_kernel, n_feat),
        sds((outputs, share), BF),
        [meta] + coarse_blocks + [w_coarse],
        [pltpu.VMEM((total, share), BF)],
    )
    given, places, last, first = gather_dom(folded, last, first)
    up = [(i, (i + 1) % n_dom) for i in range(n_dom)]
    left = lax.ppermute(last, "dom", up)
    right = lax.ppermute(first, "dom", [(j, i) for i, j in up])
    ext, one = call(
        functools.partial(hop_one_kernel, n_feat, tile),
        [sds((total, rows + 4 * tile), BF), sds((total, rows + 2 * tile), BF)],
        [meta] + blocks + [left, right, band],
        flops=2 * total * rows * kb * tile,
        bytes_accessed=8 * total * rows,
    )
    partial = call(
        functools.partial(hop_two_kernel, tile),
        sds((outputs, rows), F32),
        [ext, one, band, w_own],
        flops=2 * total * rows * (kb * tile + 3 * outputs),
        bytes_accessed=8 * total * rows,
    )
    return call(
        functools.partial(final_kernel, places, len(given), share, tile),
        sds((channels, rows), BF),
        [meta, coarse_at]
        + given
        + [coarse_tiles, ids, partial, terms, inputs, state],
        [pltpu.VMEM((outputs, clusters), BF)] * 2,
        flops=2 * outputs * rows * clusters,
        bytes_accessed=8 * outputs * rows,
    )


def solution(mesh):
    return jax.shard_map(
        body,
        mesh=mesh,
        in_specs=(
            P("feat", "dom"),
            P(None, "dom"),
            P("dom", None, None, None),
            P("dom", None),
            P("dom"),
            P("dom"),
            P(None, "feat", None, None),
            P(None, "feat", None),
            P(None, "feat"),
            P("feat", None, None),
            P("feat", None, None),
            P("feat", None, None),
            P(),
            P(),
        ),
        out_specs=P("feat", "dom"),
        check_vma=False,
    )
```

```python
import functools

import jax
import jax.numpy as jnp
from jax import lax
from jax.experimental import pallas as pl
from jax.experimental.pallas import tpu as pltpu
from jax.sharding import PartitionSpec as P

BF = jnp.bfloat16
F32 = jnp.float32
VMEM = pl.BlockSpec(memory_space=pltpu.VMEM)
SMEM = pl.BlockSpec(memory_space=pltpu.SMEM)
COUNT_ROWS = 16


def call(kernel, outs, ins, scratch=(), flops=0, bytes_accessed=0, mib=16):
    specs = [SMEM if x.dtype == jnp.int32 and x.ndim == 1 else VMEM for x in ins]
    return pl.pallas_call(
        kernel,
        out_shape=outs,
        in_specs=specs,
        out_specs=jax.tree.map(lambda _: VMEM, outs),
        scratch_shapes=list(scratch),
        compiler_params=pltpu.CompilerParams(vmem_limit_bytes=mib * 2**20),
        cost_estimate=pl.CostEstimate(
            flops=int(flops), bytes_accessed=int(bytes_accessed), transcendentals=0
        ),
    )(*ins)


def one_hot(ids, first, width):
    rel = jnp.clip(ids - first, -1, width).astype(F32).astype(BF)
    rows = lax.broadcasted_iota(jnp.int32, (width, ids.shape[1]), 0).astype(F32).astype(BF)
    return jnp.where(rel == rows, jnp.ones((), BF), jnp.zeros((), BF))


def split_counts(rows, counts):
    high = jnp.floor(counts * (1.0 / 256.0))
    row = lax.broadcasted_iota(jnp.int32, (rows, counts.shape[1]), 0)
    return jnp.where(row == 0, high, counts - 256.0 * high).astype(BF)


def join_counts(rows):
    return 256.0 * rows[0:1] + rows[1:2]


def sums_kernel(share, meta, state, ids, kept, sent, lhs):
    channels, sensors = state.shape
    lhs[:channels] = state[...]
    lhs[channels:] = jnp.ones((COUNT_ROWS, sensors), BF)
    position = lax.broadcasted_iota(jnp.int32, (1, sensors), 1)
    own = jnp.where(position < meta[1], ids[...], -1)
    for e in range(kept.shape[0]):
        for other in (1, 0):
            hot = one_hot(own, (meta[0] ^ (2 * e + other)) * share, share)
            sums = lax.dot_general(
                lhs[...], hot, (((1,), (1,)), ((), ())), preferred_element_type=F32
            )
            if other:
                sent[e, :channels] = sums[:channels].astype(BF)
                sent[e, channels:] = split_counts(COUNT_ROWS, sums[channels:])
            else:
                kept[e] = sums


def pair_kernel(kept, arrived, own, *outs):
    channels = own.shape[0] - COUNT_ROWS
    for e, out in enumerate((own,) + outs):
        came = arrived[e].astype(F32)
        sums = kept[e, :channels] + came[:channels]
        counts = kept[e, channels:] + join_counts(came[channels:])
        out[:channels] = sums.astype(out.dtype)
        out[channels:] = split_counts(COUNT_ROWS, counts).astype(out.dtype)


def split3(x):
    high = x.astype(BF)
    rest = x - high.astype(F32)
    mid = rest.astype(BF)
    return high, mid, (rest - mid.astype(F32)).astype(BF)


def pool_kernel(pieces, w_value, *refs):
    blocks, (pooled, values) = refs[:pieces], refs[pieces:]
    channels = pooled.shape[0]
    total = blocks[0][...].astype(F32)
    for ref in blocks[1:]:
        total = total + ref[...].astype(F32)
    counts = join_counts(total[channels:])
    mean = total[:channels] / jnp.maximum(counts, 1.0)
    pooled[...] = mean
    heads, size = w_value.shape[0], w_value.shape[1]
    for h in range(heads):
        out = jnp.zeros((size, mean.shape[1]), F32)
        for part in split3(mean[h * size : (h + 1) * size]):
            out = out + jnp.dot(w_value[h], part, preferred_element_type=F32)
        values[h * size : (h + 1) * size] = out.astype(BF)


def weights_kernel(share, source, target, weights):
    heads, _, clusters = target.shape
    for h in range(heads):
        s_hi, s_mid, s_lo = split3(source[h])
        t_hi, t_mid, t_lo = split3(target[h])
        left = jnp.concatenate([t_hi, t_hi, t_mid, t_hi, t_lo, t_mid], axis=0)
        right = jnp.concatenate([s_hi, s_mid, s_hi, s_lo, s_hi, s_mid], axis=0)
        scores = lax.dot_general(left, right, (((0,), (0,)), ((), ())), preferred_element_type=F32)
        scores = jnp.maximum(scores, 0.0)
        raised = jnp.exp(scores - jnp.max(scores, axis=0, keepdims=True))
        scale = 1.0 / jnp.sum(raised, axis=0, keepdims=True)
        weights[h] = (raised * scale).astype(BF)


def attend_kernel(values, weights, pooled, out):
    heads, _, share = weights.shape
    parts, channels, _ = values.shape
    size = channels // heads
    for h in range(heads):
        rows = slice(h * size, (h + 1) * size)
        every = jnp.concatenate([values[p, rows] for p in range(parts)], axis=1)
        attended = jnp.dot(every, weights[h], preferred_element_type=F32)
        out[rows] = (pooled[rows] + attended).astype(BF)


def fold_kernel(blocks, meta, *refs):
    parts, (w, out, coarse) = refs[:blocks], refs[blocks:]
    channels = parts[0].shape[0]
    for k, part in enumerate(parts):
        coarse[pl.ds(pl.multiple_of((meta[2] ^ k) * channels, channels), channels)] = part[...]
    out[...] = jnp.dot(w[...], coarse[...], preferred_element_type=F32).astype(BF)


def band_kernel(meta, cols, adj, terms, band, edge_last, edge_first, terms_out, total):
    tiles, kb, tile, _ = adj.shape
    terms_out[...] = terms[...]

    def step(t, _):
        spot = lax.broadcasted_iota(jnp.int32, (1, tile), 1) + t * tile
        total[: 2 * tile] = jnp.zeros((2 * tile, tile), F32)
        total[2 * tile :] = adj[t, kb - 1].astype(F32)
        for k in range(kb - 1):
            at = pl.ds(pl.multiple_of((cols[t * kb + k] - t) * tile, tile), tile)
            total[at] = total[at] + adj[t, k].astype(F32)
        band[t] = jnp.where(spot < meta[1], total[...], 0.0).astype(BF)
        return 0

    lax.fori_loop(0, tiles, step, 0)
    half = 3 * tile // 2
    for edge, t in ((edge_last, tiles - 1), (edge_first, 0)):
        edge[:, :tile] = band[t, :half]
        edge[:, tile:] = band[t, half:]


def pair_weights(tile, a, b):
    none = jnp.zeros((tile, tile), BF)
    return jnp.concatenate(
        [jnp.concatenate([a, none], axis=0), jnp.concatenate([none, b], axis=0)], axis=1
    )


def is_end(feat):
    return (feat + 1) % 4 < 2


def edge_kernel(n, tile, meta, *refs):
    *parts, edge_last, edge_first, last, first = refs
    channels, rows = parts[0].shape
    position = lax.broadcasted_iota(jnp.int32, (1, 2 * tile), 1)
    ends = (last, rows - 2 * tile, edge_last), (first, 0, edge_first)
    for out, start, weights in ends:
        keep = position + start < meta[1]
        for k in range(n):
            part = parts[k][:, start : start + 2 * tile]
            if k == 3 and len(parts) > n:
                other = parts[4][:, start : start + 2 * tile]
                part = jnp.where(is_end(meta[2]), other, part)
            at = pl.ds(pl.multiple_of((meta[2] ^ k) * channels, channels), channels)
            out[at] = jnp.where(keep, part, jnp.zeros((), BF))
        out[n * channels :] = weights[...]


def hop(source, at, tile, a, b):
    picked = source[:, at : at + 4 * tile]
    return jnp.dot(picked, pair_weights(tile, a, b), preferred_element_type=F32).astype(BF)


def gate_sums(w, state, one, two):
    acc = jnp.dot(w[0], state, preferred_element_type=F32)
    acc = acc + jnp.dot(w[1], one, preferred_element_type=F32)
    return acc + jnp.dot(w[2], two, preferred_element_type=F32)


def inner_kernel(n, tile, meta, *refs):
    *parts, band, w, out, state_rim, one_rim, own, one = refs
    channels, rows = parts[0].shape
    tiles = rows // tile
    pair = 2 * tile
    keep = lax.broadcasted_iota(jnp.int32, (1, rows), 1) < meta[1]
    for k in range(n):
        at = pl.ds(pl.multiple_of((meta[2] ^ k) * channels, channels), channels)
        part = parts[k][...]
        if k == 3 and len(parts) > n:
            part = jnp.where(is_end(meta[2]), parts[4][...], part)
        own[at] = jnp.where(keep, part, jnp.zeros((), BF))
    state_rim[:, :pair] = own[:, :pair]
    state_rim[:, pair:] = own[:, rows - pair :]
    for u in range(1, tiles // 2):
        made = hop(own, (2 * u - 2) * tile, tile, band[2 * u - 1], band[2 * u])
        one[:, (u - 1) * pair : u * pair] = made
    one_rim[:, :pair] = one[:, :pair]
    one_rim[:, pair:] = one[:, rows - 2 * pair :]
    for u in range(1, tiles // 2 - 1):
        at = (u - 1) * pair
        two = hop(one, at, tile, band[2 * u], band[2 * u + 1])
        state = own[:, u * pair : (u + 1) * pair]
        out[:, at : at + pair] = gate_sums(w, state, one[:, at + tile : at + tile + pair], two)


def rim_kernel(tile, left, right, state_rim, one_rim, band, w, out):
    total = state_rim.shape[0]
    half = 3 * tile // 2
    pair = 2 * tile
    tiles = band.shape[0]

    def edge(ref):
        return jnp.concatenate(
            [ref[total : total + half, :tile], ref[total : total + half, tile:]], axis=0
        )

    near = jnp.concatenate([left[:total], state_rim[:, :pair]], axis=1)
    one = jnp.concatenate([hop(near, 0, tile, edge(left), band[0]), one_rim[:, :pair]], axis=1)
    two = hop(one, 0, tile, band[0], band[1])
    out[:, :pair] = gate_sums(w, state_rim[:, :pair], one[:, tile : tile + pair], two)
    near = jnp.concatenate([state_rim[:, pair:], right[:total]], axis=1)
    made = hop(near, 0, tile, band[tiles - 1], edge(right))
    one = jnp.concatenate([one_rim[:, pair:], made], axis=1)
    two = hop(one, 0, tile, band[tiles - 2], band[tiles - 1])
    out[:, pair:] = gate_sums(w, state_rim[:, pair:], one[:, tile : tile + pair], two)


def final_kernel(places, n_given, share, tile, meta, ccols, *refs):
    given = refs[:n_given]
    ctiles, ids, middle, rim, terms, inputs, state, out, coarse, mixed = refs[n_given:]
    outputs = coarse.shape[0]
    clusters = coarse.shape[1]
    for ref, src, dst, rows, b, absolute in places:
        owner = b if absolute else meta[0] ^ b
        at = pl.ds(pl.multiple_of(owner * share, share), share)
        coarse[dst : dst + rows, at] = given[ref][src : src + rows]
    kc = ctiles.shape[1]

    def mix(t, _):
        picked = jnp.concatenate(
            [
                coarse[:, pl.ds(pl.multiple_of(ccols[t * kc + k] * tile, tile), tile)]
                for k in range(kc)
            ],
            axis=1,
        )
        at = pl.ds(pl.multiple_of(t * tile, tile), tile)
        made = jnp.dot(picked, ctiles[t].reshape(kc * tile, tile), preferred_element_type=F32)
        mixed[:, at] = (coarse[:, at].astype(F32) + made).astype(BF)
        return 0

    lax.fori_loop(0, clusters // tile, mix, 0, unroll=True)
    sensors = state.shape[1]
    channels = state.shape[0]
    width = 4 * tile

    pair = 2 * tile
    for start in range(0, sensors, width):
        at = slice(start, start + width)
        own = ids[:, at]
        hot = jnp.concatenate(
            [one_hot(own, f, share) for f in range(0, clusters, share)], axis=0
        )
        before = [middle[:, max(start - pair, 0) : min(start + width, sensors - pair) - pair]]
        if start == 0:
            before = [rim[:, :pair]] + before
        if start + width == sensors:
            before = before + [rim[:, pair:]]
        sums = jnp.concatenate(before, axis=1) + jnp.dot(mixed[...], hot, preferred_element_type=F32)
        x = inputs[:, at].astype(F32)
        given_terms = terms[:, 2:3] + terms[:, 0:1] * x[0:1] + terms[:, 1:2] * x[1:2]
        update = jax.nn.sigmoid(given_terms[:channels] + sums[:channels])
        reset = jax.nn.sigmoid(
            given_terms[channels : 2 * channels] + sums[channels : 2 * channels]
        )
        candidate = jnp.tanh(given_terms[2 * channels :] + reset * sums[2 * channels :])
        old = state[:, at].astype(F32)
        spot = lax.broadcasted_iota(jnp.int32, (1, width), 1) + start
        new = update * old + (1.0 - update) * candidate
        out[:, at] = jnp.where(spot < meta[1], new, 0.0).astype(BF)


def flip(n, b):
    return [(i, i ^ b) for i in range(n)]


def swap(array, axis, b):
    return lax.ppermute(array, axis, flip(lax.axis_size(axis), b))


def gather_dom(block, *ready):
    n = lax.axis_size("dom")
    rows = block.shape[0]
    send = lambda x, b: swap(x, "dom", b)
    if n != 8:
        every = lax.all_gather(block, "dom", axis=0, tiled=True)
        return [every], [(0, b * rows, 0, rows, b, True) for b in range(n)], *ready
    half = rows // 2
    beside = send(block, 2)
    behind = send(block, 4)
    core = send(block, 1)
    (beside, behind), ready = lax.optimization_barrier(((beside, behind), ready))
    top = send(beside[:half], 4)
    bottom = send(behind[half:], 2)
    other = send(jnp.concatenate([beside, behind, top, bottom], axis=0), 1)
    places = [
        (0, 0, 0, rows, 0, False),
        (1, 0, 0, rows, 1, False),
        (2, 0, 0, rows, 2, False),
        (3, 0, 0, rows, 4, False),
        (4, 0, 0, half, 6, False),
        (5, 0, half, half, 6, False),
        (6, 0, 0, rows, 3, False),
        (6, rows, 0, rows, 5, False),
        (6, 2 * rows, 0, rows, 7, False),
    ]
    return [block, core, beside, behind, top, bottom, other], places, *ready


def body(
    state,
    inputs,
    adj_tiles,
    adj_cols,
    valid_rows,
    cluster_of,
    w_gates,
    w_input,
    bias,
    w_value,
    source_emb,
    target_emb,
    coarse_tiles,
    coarse_cols,
):
    channels, rows = state.shape
    clusters = source_emb.shape[2]
    n_dom, n_feat = lax.axis_size("dom"), lax.axis_size("feat")
    share = clusters // n_dom
    tiles, kb, tile, _ = adj_tiles.shape
    me, feat = lax.axis_index("dom"), lax.axis_index("feat")
    meta = jnp.stack([me.astype(jnp.int32), valid_rows[0], feat.astype(jnp.int32)])
    ids = cluster_of[None, :]
    total = channels * n_feat
    outputs = 3 * channels
    sds = jax.ShapeDtypeStruct

    kept, sent = call(
        functools.partial(sums_kernel, share),
        [
            sds((n_dom // 2, channels + COUNT_ROWS, share), F32),
            sds((n_dom // 2, channels + COUNT_ROWS, share), BF),
        ],
        [meta, state, ids],
        [pltpu.VMEM((channels + COUNT_ROWS, rows), BF)],
        flops=2 * channels * rows * clusters * 3,
        bytes_accessed=8 * channels * rows,
    )
    line = n_feat == 4
    sent, state_far = lax.optimization_barrier((sent, state))
    far = [swap(state_far, "feat", k) for k in range(2, n_feat) if k == 2 or not line]
    pieces = call(
        pair_kernel,
        [sds((channels + COUNT_ROWS, share), F32)]
        + [sds((channels + COUNT_ROWS, share), BF)] * (n_dom // 2 - 1),
        [kept, swap(sent, "dom", 1)],
    )
    pieces, state_near, source_emb, target_emb = lax.optimization_barrier(
        (pieces, state, source_emb, target_emb)
    )
    arrived = [pieces[0]] + [swap(pieces[e], "dom", 2 * e) for e in range(1, n_dom // 2)]
    blocks = [state, swap(state_near, "feat", 1)] + far
    pad = [(0, 0), (0, -source_emb.shape[1] % 16), (0, 0)]
    source = lax.dynamic_slice_in_dim(source_emb, me * share, share, 2)
    weights = call(
        functools.partial(weights_kernel, share),
        sds((source.shape[0], clusters, share), BF),
        [jnp.pad(source, pad), jnp.pad(target_emb, pad)],
        flops=source.shape[0] * clusters * share * 4000,
    )
    arrived, weights = lax.optimization_barrier((arrived, weights))
    pooled, values = call(
        functools.partial(pool_kernel, n_dom // 2),
        [sds((channels, share), F32), sds((channels, share), BF)],
        [w_value] + arrived,
    )
    every_value = lax.all_gather(values, "dom", axis=0)
    own_coarse = call(attend_kernel, sds((channels, share), BF), [every_value, weights, pooled])

    own_coarse, w_gates, adj_tiles, w_input, coarse_cols = lax.optimization_barrier(
        (own_coarse, w_gates, adj_tiles, w_input, coarse_cols)
    )
    coarse_blocks = [own_coarse] + [swap(own_coarse, "feat", k) for k in range(1, n_feat)]
    if line:
        own_coarse, blocks[1:3], state_inner = lax.optimization_barrier(
            (own_coarse, blocks[1:3], state)
        )
        outer = lax.ppermute(blocks[2], "feat", [(1, 0), (2, 3)])
        blocks += [lax.ppermute(state_inner, "feat", [(1, 2), (2, 1)]), outer]
    w = jnp.transpose(w_gates, (2, 0, 1, 3)).reshape(4, outputs, total)
    w_own, w_coarse = w[:3], w[3]
    edge_shape = sds((3 * tile // 2, 2 * tile), BF)
    terms = jnp.concatenate(
        [w_input.reshape(outputs, -1).astype(F32), bias.reshape(outputs, 1)], axis=1
    )
    band, edge_last, edge_first, terms = call(
        band_kernel,
        [sds((tiles, 3 * tile, tile), BF), edge_shape, edge_shape, sds(terms.shape, F32)],
        [meta, adj_cols.reshape(-1), adj_tiles, terms],
        [pltpu.VMEM((3 * tile, tile), F32)],
        flops=10**9,
    )
    coarse_at = coarse_cols.reshape(-1)
    ready = (w_own, w_coarse, band, terms, coarse_at)
    coarse_blocks, ready = lax.optimization_barrier((coarse_blocks, ready))
    w_own, w_coarse, band, terms, coarse_at = ready
    message = sds((total + 3 * tile // 2, 2 * tile), BF)
    last, first = call(
        functools.partial(edge_kernel, n_feat, tile),
        [message, message],
        [meta] + blocks + [edge_last, edge_first],
    )
    folded = call(
        functools.partial(fold_kernel, n_feat),
        sds((outputs, share), BF),
        [meta] + coarse_blocks + [w_coarse],
        [pltpu.VMEM((total, share), BF)],
    )
    given, places, last, first = gather_dom(folded, last, first)
    up = [(i, (i + 1) % n_dom) for i in range(n_dom)]
    left = lax.ppermute(last, "dom", up)
    right = lax.ppermute(first, "dom", [(j, i) for i, j in up])
    pair = 2 * tile
    middle, state_rim, one_rim = call(
        functools.partial(inner_kernel, n_feat, tile),
        [sds((outputs, rows - 2 * pair), F32)] + [sds((total, 2 * pair), BF)] * 2,
        [meta] + blocks + [band, w_own],
        [pltpu.VMEM((total, rows), BF), pltpu.VMEM((total, rows - pair), BF)],
        flops=(4 * total * rows * kb * tile + 6 * total * rows * outputs) // 1,
        bytes_accessed=8 * total * rows,
    )
    rim = call(
        functools.partial(rim_kernel, tile),
        sds((outputs, 2 * pair), F32),
        [left, right, state_rim, one_rim, band, w_own],
        flops=30 * total * rows * outputs,
        bytes_accessed=total * rows,
    )
    return call(
        functools.partial(final_kernel, places, len(given), share, tile),
        sds((channels, rows), BF),
        [meta, coarse_at]
        + given
        + [coarse_tiles, ids, middle, rim, terms, inputs, state],
        [pltpu.VMEM((outputs, clusters), BF)] * 2,
        flops=2 * outputs * rows * clusters,
        bytes_accessed=8 * outputs * rows,
    )


def solution(mesh):
    return jax.shard_map(
        body,
        mesh=mesh,
        in_specs=(
            P("feat", "dom"),
            P(None, "dom"),
            P("dom", None, None, None),
            P("dom", None),
            P("dom"),
            P("dom"),
            P(None, "feat", None, None),
            P(None, "feat", None),
            P(None, "feat"),
            P("feat", None, None),
            P("feat", None, None),
            P("feat", None, None),
            P(),
            P(),
        ),
        out_specs=P("feat", "dom"),
        check_vma=False,
    )
```

```python
import functools

import jax
import jax.numpy as jnp
from jax import lax
from jax.experimental import pallas as pl
from jax.experimental.pallas import tpu as pltpu
from jax.sharding import PartitionSpec as P

BF = jnp.bfloat16
F32 = jnp.float32
VMEM = pl.BlockSpec(memory_space=pltpu.VMEM)
SMEM = pl.BlockSpec(memory_space=pltpu.SMEM)
COUNT_ROWS = 16


def call(kernel, outs, ins, scratch=(), flops=0, bytes_accessed=0, mib=16):
    specs = [SMEM if x.dtype == jnp.int32 and x.size < 1024 else VMEM for x in ins]
    return pl.pallas_call(
        kernel,
        out_shape=outs,
        in_specs=specs,
        out_specs=jax.tree.map(lambda _: VMEM, outs),
        scratch_shapes=list(scratch),
        compiler_params=pltpu.CompilerParams(vmem_limit_bytes=mib * 2**20),
        cost_estimate=pl.CostEstimate(
            flops=int(flops), bytes_accessed=int(bytes_accessed), transcendentals=0
        ),
    )(*ins)


def one_hot(ids, first, width):
    rel = jnp.clip(ids - first, -1, width).astype(F32).astype(BF)
    rows = lax.broadcasted_iota(jnp.int32, (width, ids.shape[1]), 0).astype(F32).astype(BF)
    return jnp.where(rel == rows, jnp.ones((), BF), jnp.zeros((), BF))


def split_counts(rows, counts):
    high = jnp.floor(counts * (1.0 / 256.0))
    row = lax.broadcasted_iota(jnp.int32, (rows, counts.shape[1]), 0)
    return jnp.where(row == 0, high, counts - 256.0 * high).astype(BF)


def join_counts(rows):
    return 256.0 * rows[0:1] + rows[1:2]


def sums_kernel(share, meta, state, ids, kept, sent, lhs):
    channels, sensors = state.shape
    lhs[:channels] = state[...]
    lhs[channels:] = jnp.ones((COUNT_ROWS, sensors), BF)
    position = lax.broadcasted_iota(jnp.int32, (1, sensors), 1)
    own = jnp.where(position < meta[1], ids[...], -1)
    for e in range(kept.shape[0]):
        for other in (1, 0):
            hot = one_hot(own, (meta[0] ^ (2 * e + other)) * share, share)
            sums = lax.dot_general(
                lhs[...], hot, (((1,), (1,)), ((), ())), preferred_element_type=F32
            )
            if other:
                sent[e, :channels] = sums[:channels].astype(BF)
                sent[e, channels:] = split_counts(COUNT_ROWS, sums[channels:])
            else:
                kept[e] = sums


def pair_kernel(kept, arrived, own, *outs):
    channels = own.shape[0] - COUNT_ROWS
    for e, out in enumerate((own,) + outs):
        came = arrived[e].astype(F32)
        sums = kept[e, :channels] + came[:channels]
        counts = kept[e, channels:] + join_counts(came[channels:])
        out[:channels] = sums.astype(out.dtype)
        out[channels:] = split_counts(COUNT_ROWS, counts).astype(out.dtype)


def split3(x):
    high = x.astype(BF)
    rest = x - high.astype(F32)
    mid = rest.astype(BF)
    return high, mid, (rest - mid.astype(F32)).astype(BF)


def pool_kernel(pieces, w_value, *refs):
    blocks, (pooled, values) = refs[:pieces], refs[pieces:]
    channels = pooled.shape[0]
    total = blocks[0][...].astype(F32)
    for ref in blocks[1:]:
        total = total + ref[...].astype(F32)
    counts = join_counts(total[channels:])
    mean = total[:channels] / jnp.maximum(counts, 1.0)
    pooled[...] = mean
    heads, size = w_value.shape[0], w_value.shape[1]
    for h in range(heads):
        out = jnp.zeros((size, mean.shape[1]), F32)
        for part in split3(mean[h * size : (h + 1) * size]):
            out = out + jnp.dot(w_value[h], part, preferred_element_type=F32)
        values[h * size : (h + 1) * size] = out.astype(BF)


def weights_kernel(share, source, target, weights):
    heads, _, clusters = target.shape
    for h in range(heads):
        s_hi, s_mid, s_lo = split3(source[h])
        t_hi, t_mid, t_lo = split3(target[h])
        left = jnp.concatenate([t_hi, t_hi, t_mid, t_hi, t_lo, t_mid], axis=0)
        right = jnp.concatenate([s_hi, s_mid, s_hi, s_lo, s_hi, s_mid], axis=0)
        scores = lax.dot_general(left, right, (((0,), (0,)), ((), ())), preferred_element_type=F32)
        scores = jnp.maximum(scores, 0.0)
        raised = jnp.exp(scores - jnp.max(scores, axis=0, keepdims=True))
        scale = 1.0 / jnp.sum(raised, axis=0, keepdims=True)
        weights[h] = (raised * scale).astype(BF)


def attend_kernel(values, weights, pooled, out):
    heads, _, share = weights.shape
    parts, channels, _ = values.shape
    size = channels // heads
    for h in range(heads):
        rows = slice(h * size, (h + 1) * size)
        every = jnp.concatenate([values[p, rows] for p in range(parts)], axis=1)
        attended = jnp.dot(every, weights[h], preferred_element_type=F32)
        out[rows] = (pooled[rows] + attended).astype(BF)


def fold_kernel(blocks, meta, *refs):
    parts, (w, out, coarse) = refs[:blocks], refs[blocks:]
    channels = parts[0].shape[0]
    for k, part in enumerate(parts):
        coarse[pl.ds(pl.multiple_of((meta[2] ^ k) * channels, channels), channels)] = part[...]
    out[...] = jnp.dot(w[...], coarse[...], preferred_element_type=F32).astype(BF)


def band_kernel(meta, cols, adj, terms, band, edge_last, edge_first, terms_out, total):
    tiles, kb, tile, _ = adj.shape
    terms_out[...] = terms[...]

    def step(t, _):
        spot = lax.broadcasted_iota(jnp.int32, (1, tile), 1) + t * tile
        total[: 2 * tile] = jnp.zeros((2 * tile, tile), F32)
        total[2 * tile :] = adj[t, kb - 1].astype(F32)
        for k in range(kb - 1):
            at = pl.ds(pl.multiple_of((cols[t * kb + k] - t) * tile, tile), tile)
            total[at] = total[at] + adj[t, k].astype(F32)
        band[t] = jnp.where(spot < meta[1], total[...], 0.0).astype(BF)
        return 0

    lax.fori_loop(0, tiles, step, 0)
    half = 3 * tile // 2
    for edge, t in ((edge_last, tiles - 1), (edge_first, 0)):
        edge[:, :tile] = band[t, :half]
        edge[:, tile:] = band[t, half:]


def pair_weights(tile, a, b):
    none = jnp.zeros((tile, tile), BF)
    return jnp.concatenate(
        [jnp.concatenate([a, none], axis=0), jnp.concatenate([none, b], axis=0)], axis=1
    )


def is_end(feat):
    return (feat + 1) % 4 < 2


def edge_kernel(n, tile, meta, *refs):
    *parts, edge_last, edge_first, last, first = refs
    channels, rows = parts[0].shape
    position = lax.broadcasted_iota(jnp.int32, (1, 2 * tile), 1)
    ends = (last, rows - 2 * tile, edge_last), (first, 0, edge_first)
    for out, start, weights in ends:
        keep = position + start < meta[1]
        for k in range(n):
            part = parts[k][:, start : start + 2 * tile]
            if k == 3 and len(parts) > n:
                other = parts[4][:, start : start + 2 * tile]
                part = jnp.where(is_end(meta[2]), other, part)
            at = pl.ds(pl.multiple_of((meta[2] ^ k) * channels, channels), channels)
            out[at] = jnp.where(keep, part, jnp.zeros((), BF))
        out[n * channels :] = weights[...]


def hop(source, at, tile, a, b):
    picked = source[:, at : at + 4 * tile]
    return jnp.dot(picked, pair_weights(tile, a, b), preferred_element_type=F32).astype(BF)


def gate_sums(w, state, one, two):
    acc = jnp.dot(w[0], state, preferred_element_type=F32)
    acc = acc + jnp.dot(w[1], one, preferred_element_type=F32)
    return acc + jnp.dot(w[2], two, preferred_element_type=F32)


def inner_kernel(n, tile, meta, *refs):
    *parts, band, w, out, state_rim, one_rim, own, one = refs
    channels, rows = parts[0].shape
    tiles = rows // tile
    pair = 2 * tile
    keep = lax.broadcasted_iota(jnp.int32, (1, rows), 1) < meta[1]
    for k in range(n):
        at = pl.ds(pl.multiple_of((meta[2] ^ k) * channels, channels), channels)
        part = parts[k][...]
        if k == 3 and len(parts) > n:
            part = jnp.where(is_end(meta[2]), parts[4][...], part)
        own[at] = jnp.where(keep, part, jnp.zeros((), BF))
    state_rim[:, :pair] = own[:, :pair]
    state_rim[:, pair:] = own[:, rows - pair :]
    for u in range(1, tiles // 2):
        made = hop(own, (2 * u - 2) * tile, tile, band[2 * u - 1], band[2 * u])
        one[:, (u - 1) * pair : u * pair] = made
    one_rim[:, :pair] = one[:, :pair]
    one_rim[:, pair:] = one[:, rows - 2 * pair :]
    for u in range(1, tiles // 2 - 1):
        at = (u - 1) * pair
        two = hop(one, at, tile, band[2 * u], band[2 * u + 1])
        state = own[:, u * pair : (u + 1) * pair]
        out[:, at : at + pair] = gate_sums(w, state, one[:, at + tile : at + tile + pair], two)


def rim_kernel(tile, left, right, state_rim, one_rim, band, w, out):
    total = state_rim.shape[0]
    half = 3 * tile // 2
    pair = 2 * tile
    tiles = band.shape[0]

    def edge(ref):
        return jnp.concatenate(
            [ref[total : total + half, :tile], ref[total : total + half, tile:]], axis=0
        )

    near = jnp.concatenate([left[:total], state_rim[:, :pair]], axis=1)
    one = jnp.concatenate([hop(near, 0, tile, edge(left), band[0]), one_rim[:, :pair]], axis=1)
    two = hop(one, 0, tile, band[0], band[1])
    out[:, :pair] = gate_sums(w, state_rim[:, :pair], one[:, tile : tile + pair], two)
    near = jnp.concatenate([state_rim[:, pair:], right[:total]], axis=1)
    made = hop(near, 0, tile, band[tiles - 1], edge(right))
    one = jnp.concatenate([one_rim[:, pair:], made], axis=1)
    two = hop(one, 0, tile, band[tiles - 2], band[tiles - 1])
    out[:, pair:] = gate_sums(w, state_rim[:, pair:], one[:, tile : tile + pair], two)


def final_kernel(places, n_given, share, tile, meta, ccols, *refs):
    given = refs[:n_given]
    ctiles, ids, middle, rim, terms, inputs, state, out, coarse, mixed = refs[n_given:]
    outputs = coarse.shape[0]
    clusters = coarse.shape[1]
    for ref, src, dst, rows, b, absolute in places:
        owner = b if absolute else meta[0] ^ b
        at = pl.ds(pl.multiple_of(owner * share, share), share)
        coarse[dst : dst + rows, at] = given[ref][src : src + rows]
    kc = ctiles.shape[1]

    def mix(t, _):
        picked = jnp.concatenate(
            [
                coarse[:, pl.ds(pl.multiple_of(ccols[k, t] * tile, tile), tile)]
                for k in range(kc)
            ],
            axis=1,
        )
        at = pl.ds(pl.multiple_of(t * tile, tile), tile)
        made = jnp.dot(picked, ctiles[t].reshape(kc * tile, tile), preferred_element_type=F32)
        mixed[:, at] = (coarse[:, at].astype(F32) + made).astype(BF)
        return 0

    lax.fori_loop(0, clusters // tile, mix, 0, unroll=True)
    sensors = state.shape[1]
    channels = state.shape[0]
    width = 4 * tile

    pair = 2 * tile
    for start in range(0, sensors, width):
        at = slice(start, start + width)
        own = ids[:, at]
        hot = jnp.concatenate(
            [one_hot(own, f, share) for f in range(0, clusters, share)], axis=0
        )
        before = [middle[:, max(start - pair, 0) : min(start + width, sensors - pair) - pair]]
        if start == 0:
            before = [rim[:, :pair]] + before
        if start + width == sensors:
            before = before + [rim[:, pair:]]
        sums = jnp.concatenate(before, axis=1) + jnp.dot(mixed[...], hot, preferred_element_type=F32)
        x = inputs[:, at].astype(F32)
        given_terms = terms[:, 2:3] + terms[:, 0:1] * x[0:1] + terms[:, 1:2] * x[1:2]
        update = jax.nn.sigmoid(given_terms[:channels] + sums[:channels])
        reset = jax.nn.sigmoid(
            given_terms[channels : 2 * channels] + sums[channels : 2 * channels]
        )
        candidate = jnp.tanh(given_terms[2 * channels :] + reset * sums[2 * channels :])
        old = state[:, at].astype(F32)
        spot = lax.broadcasted_iota(jnp.int32, (1, width), 1) + start
        new = update * old + (1.0 - update) * candidate
        out[:, at] = jnp.where(spot < meta[1], new, 0.0).astype(BF)


def flip(n, b):
    return [(i, i ^ b) for i in range(n)]


def swap(array, axis, b):
    return lax.ppermute(array, axis, flip(lax.axis_size(axis), b))


def gather_dom(block, *ready):
    n = lax.axis_size("dom")
    rows = block.shape[0]
    send = lambda x, b: swap(x, "dom", b)
    if n != 8:
        every = lax.all_gather(block, "dom", axis=0, tiled=True)
        return [every], [(0, b * rows, 0, rows, b, True) for b in range(n)], *ready
    half = rows // 2
    beside = send(block, 2)
    behind = send(block, 4)
    core = send(block, 1)
    (beside, behind), ready = lax.optimization_barrier(((beside, behind), ready))
    top = send(beside[:half], 4)
    bottom = send(behind[half:], 2)
    other = send(jnp.concatenate([beside, behind, top, bottom], axis=0), 1)
    places = [
        (0, 0, 0, rows, 0, False),
        (1, 0, 0, rows, 1, False),
        (2, 0, 0, rows, 2, False),
        (3, 0, 0, rows, 4, False),
        (4, 0, 0, half, 6, False),
        (5, 0, half, half, 6, False),
        (6, 0, 0, rows, 3, False),
        (6, rows, 0, rows, 5, False),
        (6, 2 * rows, 0, rows, 7, False),
    ]
    return [block, core, beside, behind, top, bottom, other], places, *ready


def body(
    state,
    inputs,
    adj_tiles,
    adj_cols,
    valid_rows,
    cluster_of,
    w_gates,
    w_input,
    bias,
    w_value,
    source_emb,
    target_emb,
    coarse_tiles,
    coarse_cols,
):
    channels, rows = state.shape
    clusters = source_emb.shape[2]
    n_dom, n_feat = lax.axis_size("dom"), lax.axis_size("feat")
    share = clusters // n_dom
    tiles, kb, tile, _ = adj_tiles.shape
    me, feat = lax.axis_index("dom"), lax.axis_index("feat")
    meta = jnp.stack([me.astype(jnp.int32), valid_rows[0], feat.astype(jnp.int32)])
    ids = cluster_of[None, :]
    total = channels * n_feat
    outputs = 3 * channels
    sds = jax.ShapeDtypeStruct

    kept, sent = call(
        functools.partial(sums_kernel, share),
        [
            sds((n_dom // 2, channels + COUNT_ROWS, share), F32),
            sds((n_dom // 2, channels + COUNT_ROWS, share), BF),
        ],
        [meta, state, ids],
        [pltpu.VMEM((channels + COUNT_ROWS, rows), BF)],
        flops=2 * channels * rows * clusters * 3,
        bytes_accessed=8 * channels * rows,
    )
    line = n_feat == 4
    sent, state_far = lax.optimization_barrier((sent, state))
    far = [swap(state_far, "feat", k) for k in range(2, n_feat) if k == 2 or not line]
    pieces = call(
        pair_kernel,
        [sds((channels + COUNT_ROWS, share), F32)]
        + [sds((channels + COUNT_ROWS, share), BF)] * (n_dom // 2 - 1),
        [kept, swap(sent, "dom", 1)],
    )
    pieces, state_near, source_emb, target_emb = lax.optimization_barrier(
        (pieces, state, source_emb, target_emb)
    )
    arrived = [pieces[0]] + [swap(pieces[e], "dom", 2 * e) for e in range(1, n_dom // 2)]
    blocks = [state, swap(state_near, "feat", 1)] + far
    pad = [(0, 0), (0, -source_emb.shape[1] % 16), (0, 0)]
    source = lax.dynamic_slice_in_dim(source_emb, me * share, share, 2)
    weights = call(
        functools.partial(weights_kernel, share),
        sds((source.shape[0], clusters, share), BF),
        [jnp.pad(source, pad), jnp.pad(target_emb, pad)],
        flops=source.shape[0] * clusters * share * 4000,
    )
    arrived, weights = lax.optimization_barrier((arrived, weights))
    pooled, values = call(
        functools.partial(pool_kernel, n_dom // 2),
        [sds((channels, share), F32), sds((channels, share), BF)],
        [w_value] + arrived,
    )
    every_value = lax.all_gather(values, "dom", axis=0)
    own_coarse = call(attend_kernel, sds((channels, share), BF), [every_value, weights, pooled])

    own_coarse, w_gates, adj_cols, w_input, coarse_cols = lax.optimization_barrier(
        (own_coarse, w_gates, adj_cols, w_input, coarse_cols)
    )
    coarse_blocks = [own_coarse] + [swap(own_coarse, "feat", k) for k in range(1, n_feat)]
    if line:
        own_coarse, blocks[1:3], state_inner = lax.optimization_barrier(
            (own_coarse, blocks[1:3], state)
        )
        outer = lax.ppermute(blocks[2], "feat", [(1, 0), (2, 3)])
        blocks += [lax.ppermute(state_inner, "feat", [(1, 2), (2, 1)]), outer]
    w = jnp.transpose(w_gates, (2, 0, 1, 3)).reshape(4, outputs, total)
    w_own, w_coarse = w[:3], w[3]
    edge_shape = sds((3 * tile // 2, 2 * tile), BF)
    terms = jnp.concatenate(
        [w_input.reshape(outputs, -1).astype(F32), bias.reshape(outputs, 1)], axis=1
    )
    band, edge_last, edge_first, terms = call(
        band_kernel,
        [sds((tiles, 3 * tile, tile), BF), edge_shape, edge_shape, sds(terms.shape, F32)],
        [meta, adj_cols.reshape(-1), adj_tiles, terms],
        [pltpu.VMEM((3 * tile, tile), F32)],
        flops=10**9,
    )
    coarse_at = coarse_cols.T
    ready = (w_own, w_coarse, band, terms, coarse_at)
    coarse_blocks, ready = lax.optimization_barrier((coarse_blocks, ready))
    w_own, w_coarse, band, terms, coarse_at = ready
    message = sds((total + 3 * tile // 2, 2 * tile), BF)
    last, first = call(
        functools.partial(edge_kernel, n_feat, tile),
        [message, message],
        [meta] + blocks + [edge_last, edge_first],
    )
    folded = call(
        functools.partial(fold_kernel, n_feat),
        sds((outputs, share), BF),
        [meta] + coarse_blocks + [w_coarse],
        [pltpu.VMEM((total, share), BF)],
    )
    given, places, last, first = gather_dom(folded, last, first)
    up = [(i, (i + 1) % n_dom) for i in range(n_dom)]
    left = lax.ppermute(last, "dom", up)
    right = lax.ppermute(first, "dom", [(j, i) for i, j in up])
    pair = 2 * tile
    middle, state_rim, one_rim = call(
        functools.partial(inner_kernel, n_feat, tile),
        [sds((outputs, rows - 2 * pair), F32)] + [sds((total, 2 * pair), BF)] * 2,
        [meta] + blocks + [band, w_own],
        [pltpu.VMEM((total, rows), BF), pltpu.VMEM((total, rows - pair), BF)],
        flops=(4 * total * rows * kb * tile + 6 * total * rows * outputs) // 1,
        bytes_accessed=8 * total * rows,
    )
    rim = call(
        functools.partial(rim_kernel, tile),
        sds((outputs, 2 * pair), F32),
        [left, right, state_rim, one_rim, band, w_own],
        flops=30 * total * rows * outputs,
        bytes_accessed=total * rows,
    )
    return call(
        functools.partial(final_kernel, places, len(given), share, tile),
        sds((channels, rows), BF),
        [meta, coarse_at]
        + given
        + [coarse_tiles, ids, middle, rim, terms, inputs, state],
        [pltpu.VMEM((outputs, clusters), BF)] * 2,
        flops=2 * outputs * rows * clusters,
        bytes_accessed=8 * outputs * rows,
    )


def solution(mesh):
    return jax.shard_map(
        body,
        mesh=mesh,
        in_specs=(
            P("feat", "dom"),
            P(None, "dom"),
            P("dom", None, None, None),
            P("dom", None),
            P("dom"),
            P("dom"),
            P(None, "feat", None, None),
            P(None, "feat", None),
            P(None, "feat"),
            P("feat", None, None),
            P("feat", None, None),
            P("feat", None, None),
            P(),
            P(),
        ),
        out_specs=P("feat", "dom"),
        check_vma=False,
    )
```

```python
import functools

import jax
import jax.numpy as jnp
from jax import lax
from jax.experimental import pallas as pl
from jax.experimental.pallas import tpu as pltpu
from jax.sharding import PartitionSpec as P

BF = jnp.bfloat16
F32 = jnp.float32
VMEM = pl.BlockSpec(memory_space=pltpu.VMEM)
SMEM = pl.BlockSpec(memory_space=pltpu.SMEM)
COUNT_ROWS = 16


def call(kernel, outs, ins, scratch=(), flops=0, bytes_accessed=0, mib=16):
    specs = [SMEM if x.dtype == jnp.int32 and x.size < 1024 else VMEM for x in ins]
    return pl.pallas_call(
        kernel,
        out_shape=outs,
        in_specs=specs,
        out_specs=jax.tree.map(lambda _: VMEM, outs),
        scratch_shapes=list(scratch),
        compiler_params=pltpu.CompilerParams(vmem_limit_bytes=mib * 2**20),
        cost_estimate=pl.CostEstimate(
            flops=int(flops), bytes_accessed=int(bytes_accessed), transcendentals=0
        ),
    )(*ins)


def one_hot(ids, first, width):
    rel = jnp.clip(ids - first, -1, width).astype(F32).astype(BF)
    rows = lax.broadcasted_iota(jnp.int32, (width, ids.shape[1]), 0).astype(F32).astype(BF)
    return jnp.where(rel == rows, jnp.ones((), BF), jnp.zeros((), BF))


def split_counts(rows, counts):
    high = jnp.floor(counts * (1.0 / 256.0))
    row = lax.broadcasted_iota(jnp.int32, (rows, counts.shape[1]), 0)
    return jnp.where(row == 0, high, counts - 256.0 * high).astype(BF)


def join_counts(rows):
    return 256.0 * rows[0:1] + rows[1:2]


def sums_kernel(share, meta, state, ids, kept, sent, lhs):
    channels, sensors = state.shape
    lhs[:channels] = state[...]
    lhs[channels:] = jnp.ones((COUNT_ROWS, sensors), BF)
    position = lax.broadcasted_iota(jnp.int32, (1, sensors), 1)
    own = jnp.where(position < meta[1], ids[...], -1)
    for e in range(kept.shape[0]):
        for other in (1, 0):
            hot = one_hot(own, (meta[0] ^ (2 * e + other)) * share, share)
            sums = lax.dot_general(
                lhs[...], hot, (((1,), (1,)), ((), ())), preferred_element_type=F32
            )
            if other:
                sent[e, :channels] = sums[:channels].astype(BF)
                sent[e, channels:] = split_counts(COUNT_ROWS, sums[channels:])
            else:
                kept[e] = sums


def pair_kernel(kept, arrived, own, *outs):
    channels = own.shape[0] - COUNT_ROWS
    for e, out in enumerate((own,) + outs):
        came = arrived[e].astype(F32)
        sums = kept[e, :channels] + came[:channels]
        counts = kept[e, channels:] + join_counts(came[channels:])
        out[:channels] = sums.astype(out.dtype)
        out[channels:] = split_counts(COUNT_ROWS, counts).astype(out.dtype)


def split3(x):
    high = x.astype(BF)
    rest = x - high.astype(F32)
    mid = rest.astype(BF)
    return high, mid, (rest - mid.astype(F32)).astype(BF)


def pool_kernel(pieces, w_value, *refs):
    blocks, (pooled, values) = refs[:pieces], refs[pieces:]
    channels = pooled.shape[0]
    total = blocks[0][...].astype(F32)
    for ref in blocks[1:]:
        total = total + ref[...].astype(F32)
    counts = join_counts(total[channels:])
    mean = total[:channels] / jnp.maximum(counts, 1.0)
    pooled[...] = mean
    heads, size = w_value.shape[0], w_value.shape[1]
    for h in range(heads):
        out = jnp.zeros((size, mean.shape[1]), F32)
        for part in split3(mean[h * size : (h + 1) * size]):
            out = out + jnp.dot(w_value[h], part, preferred_element_type=F32)
        values[h * size : (h + 1) * size] = out.astype(BF)


def weights_kernel(share, source, target, weights):
    heads, _, clusters = target.shape
    for h in range(heads):
        s_hi, s_mid, s_lo = split3(source[h])
        t_hi, t_mid, t_lo = split3(target[h])
        left = jnp.concatenate([t_hi, t_hi, t_mid, t_hi, t_lo, t_mid], axis=0)
        right = jnp.concatenate([s_hi, s_mid, s_hi, s_lo, s_hi, s_mid], axis=0)
        scores = lax.dot_general(left, right, (((0,), (0,)), ((), ())), preferred_element_type=F32)
        scores = jnp.maximum(scores, 0.0)
        raised = jnp.exp(scores - jnp.max(scores, axis=0, keepdims=True))
        scale = 1.0 / jnp.sum(raised, axis=0, keepdims=True)
        weights[h] = (raised * scale).astype(BF)


def attend_kernel(values, weights, pooled, out):
    heads, _, share = weights.shape
    parts, channels, _ = values.shape
    size = channels // heads
    for h in range(heads):
        rows = slice(h * size, (h + 1) * size)
        every = jnp.concatenate([values[p, rows] for p in range(parts)], axis=1)
        attended = jnp.dot(every, weights[h], preferred_element_type=F32)
        out[rows] = (pooled[rows] + attended).astype(BF)


def fold_kernel(blocks, meta, *refs):
    parts, (w, out, coarse) = refs[:blocks], refs[blocks:]
    channels = parts[0].shape[0]
    for k, part in enumerate(parts):
        coarse[pl.ds(pl.multiple_of((meta[2] ^ k) * channels, channels), channels)] = part[...]
    out[...] = jnp.dot(w[...], coarse[...], preferred_element_type=F32).astype(BF)


def band_kernel(meta, cols, adj, terms, band, edge_last, edge_first, terms_out, total):
    tiles, kb, tile, _ = adj.shape
    terms_out[...] = terms[...]

    def step(t, _):
        spot = lax.broadcasted_iota(jnp.int32, (1, tile), 1) + t * tile
        total[: 2 * tile] = jnp.zeros((2 * tile, tile), F32)
        total[2 * tile :] = adj[t, kb - 1].astype(F32)
        for k in range(kb - 1):
            at = pl.ds(pl.multiple_of((cols[t * kb + k] - t) * tile, tile), tile)
            total[at] = total[at] + adj[t, k].astype(F32)
        band[t] = jnp.where(spot < meta[1], total[...], 0.0).astype(BF)
        return 0

    lax.fori_loop(0, tiles, step, 0)
    half = 3 * tile // 2
    for edge, t in ((edge_last, tiles - 1), (edge_first, 0)):
        edge[:, :tile] = band[t, :half]
        edge[:, tile:] = band[t, half:]


def pair_weights(tile, a, b):
    none = jnp.zeros((tile, tile), BF)
    return jnp.concatenate(
        [jnp.concatenate([a, none], axis=0), jnp.concatenate([none, b], axis=0)], axis=1
    )


def is_end(feat):
    return (feat + 1) % 4 < 2


def edge_kernel(n, tile, meta, *refs):
    *parts, edge_last, edge_first, last, first = refs
    channels, rows = parts[0].shape
    position = lax.broadcasted_iota(jnp.int32, (1, 2 * tile), 1)
    ends = (last, rows - 2 * tile, edge_last), (first, 0, edge_first)
    for out, start, weights in ends:
        keep = position + start < meta[1]
        for k in range(n):
            part = parts[k][:, start : start + 2 * tile]
            if k == 3 and len(parts) > n:
                other = parts[4][:, start : start + 2 * tile]
                part = jnp.where(is_end(meta[2]), other, part)
            at = pl.ds(pl.multiple_of((meta[2] ^ k) * channels, channels), channels)
            out[at] = jnp.where(keep, part, jnp.zeros((), BF))
        out[n * channels :] = weights[...]


def hop(source, at, tile, a, b):
    picked = source[:, at : at + 4 * tile]
    return jnp.dot(picked, pair_weights(tile, a, b), preferred_element_type=F32).astype(BF)


def gate_sums(w, state, one, two):
    acc = jnp.dot(w[0], state, preferred_element_type=F32)
    acc = acc + jnp.dot(w[1], one, preferred_element_type=F32)
    return acc + jnp.dot(w[2], two, preferred_element_type=F32)


def inner_kernel(n, tile, meta, *refs):
    *parts, band, w, out, state_rim, one_rim, own, one = refs
    channels, rows = parts[0].shape
    tiles = rows // tile
    pair = 2 * tile
    keep = lax.broadcasted_iota(jnp.int32, (1, rows), 1) < meta[1]
    for k in range(n):
        at = pl.ds(pl.multiple_of((meta[2] ^ k) * channels, channels), channels)
        part = parts[k][...]
        if k == 3 and len(parts) > n:
            part = jnp.where(is_end(meta[2]), parts[4][...], part)
        own[at] = jnp.where(keep, part, jnp.zeros((), BF))
    state_rim[:, :pair] = own[:, :pair]
    state_rim[:, pair:] = own[:, rows - pair :]
    for u in range(1, tiles // 2):
        made = hop(own, (2 * u - 2) * tile, tile, band[2 * u - 1], band[2 * u])
        one[:, (u - 1) * pair : u * pair] = made
    one_rim[:, :pair] = one[:, :pair]
    one_rim[:, pair:] = one[:, rows - 2 * pair :]
    for u in range(1, tiles // 2 - 1):
        at = (u - 1) * pair
        two = hop(one, at, tile, band[2 * u], band[2 * u + 1])
        state = own[:, u * pair : (u + 1) * pair]
        out[:, at : at + pair] = gate_sums(w, state, one[:, at + tile : at + tile + pair], two)


def rim_kernel(tile, left, right, state_rim, one_rim, band, w, out):
    total = state_rim.shape[0]
    half = 3 * tile // 2
    pair = 2 * tile
    tiles = band.shape[0]

    def edge(ref):
        return jnp.concatenate(
            [ref[total : total + half, :tile], ref[total : total + half, tile:]], axis=0
        )

    near = jnp.concatenate([left[:total], state_rim[:, :pair]], axis=1)
    one = jnp.concatenate([hop(near, 0, tile, edge(left), band[0]), one_rim[:, :pair]], axis=1)
    two = hop(one, 0, tile, band[0], band[1])
    out[:, :pair] = gate_sums(w, state_rim[:, :pair], one[:, tile : tile + pair], two)
    near = jnp.concatenate([state_rim[:, pair:], right[:total]], axis=1)
    made = hop(near, 0, tile, band[tiles - 1], edge(right))
    one = jnp.concatenate([one_rim[:, pair:], made], axis=1)
    two = hop(one, 0, tile, band[tiles - 2], band[tiles - 1])
    out[:, pair:] = gate_sums(w, state_rim[:, pair:], one[:, tile : tile + pair], two)


def final_kernel(places, n_given, share, tile, meta, ccols, *refs):
    given = refs[:n_given]
    ctiles, ids, middle, rim, terms, inputs, state, out, coarse, mixed = refs[n_given:]
    outputs = coarse.shape[0]
    clusters = coarse.shape[1]
    for ref, src, dst, rows, b, absolute in places:
        owner = b if absolute else meta[0] ^ b
        at = pl.ds(pl.multiple_of(owner * share, share), share)
        coarse[dst : dst + rows, at] = given[ref][src : src + rows]
    kc = ctiles.shape[1]

    def mix(t, _):
        picked = jnp.concatenate(
            [
                coarse[:, pl.ds(pl.multiple_of(ccols[k, t] * tile, tile), tile)]
                for k in range(kc)
            ],
            axis=1,
        )
        at = pl.ds(pl.multiple_of(t * tile, tile), tile)
        made = jnp.dot(picked, ctiles[t].reshape(kc * tile, tile), preferred_element_type=F32)
        mixed[:, at] = (coarse[:, at].astype(F32) + made).astype(BF)
        return 0

    lax.fori_loop(0, clusters // tile, mix, 0, unroll=True)
    sensors = state.shape[1]
    channels = state.shape[0]
    width = 4 * tile

    pair = 2 * tile
    for start in range(0, sensors, width):
        at = slice(start, start + width)
        own = ids[:, at]
        hot = jnp.concatenate(
            [one_hot(own, f, share) for f in range(0, clusters, share)], axis=0
        )
        before = [middle[:, max(start - pair, 0) : min(start + width, sensors - pair) - pair]]
        if start == 0:
            before = [rim[:, :pair]] + before
        if start + width == sensors:
            before = before + [rim[:, pair:]]
        sums = jnp.concatenate(before, axis=1) + jnp.dot(mixed[...], hot, preferred_element_type=F32)
        x = inputs[:, at].astype(F32)
        given_terms = terms[:, 2:3] + terms[:, 0:1] * x[0:1] + terms[:, 1:2] * x[1:2]
        update = jax.nn.sigmoid(given_terms[:channels] + sums[:channels])
        reset = jax.nn.sigmoid(
            given_terms[channels : 2 * channels] + sums[channels : 2 * channels]
        )
        candidate = jnp.tanh(given_terms[2 * channels :] + reset * sums[2 * channels :])
        old = state[:, at].astype(F32)
        spot = lax.broadcasted_iota(jnp.int32, (1, width), 1) + start
        new = update * old + (1.0 - update) * candidate
        out[:, at] = jnp.where(spot < meta[1], new, 0.0).astype(BF)


def flip(n, b):
    return [(i, i ^ b) for i in range(n)]


def swap(array, axis, b):
    return lax.ppermute(array, axis, flip(lax.axis_size(axis), b))


def gather_dom(block, *ready):
    n = lax.axis_size("dom")
    rows = block.shape[0]
    send = lambda x, b: swap(x, "dom", b)
    if n != 8:
        every = lax.all_gather(block, "dom", axis=0, tiled=True)
        return [every], [(0, b * rows, 0, rows, b, True) for b in range(n)], *ready
    half = rows // 2
    beside = send(block, 2)
    behind = send(block, 4)
    core = send(block, 1)
    (beside, behind), ready = lax.optimization_barrier(((beside, behind), ready))
    top = send(beside[:half], 4)
    bottom = send(behind[half:], 2)
    other = send(jnp.concatenate([beside, behind], axis=0), 1)
    corner = send(jnp.concatenate([top, bottom], axis=0), 1)
    places = [
        (0, 0, 0, rows, 0, False),
        (1, 0, 0, rows, 1, False),
        (2, 0, 0, rows, 2, False),
        (3, 0, 0, rows, 4, False),
        (4, 0, 0, half, 6, False),
        (5, 0, half, half, 6, False),
        (6, 0, 0, rows, 3, False),
        (6, rows, 0, rows, 5, False),
        (7, 0, 0, rows, 7, False),
    ]
    return [block, core, beside, behind, top, bottom, other, corner], places, *ready


def body(
    state,
    inputs,
    adj_tiles,
    adj_cols,
    valid_rows,
    cluster_of,
    w_gates,
    w_input,
    bias,
    w_value,
    source_emb,
    target_emb,
    coarse_tiles,
    coarse_cols,
):
    channels, rows = state.shape
    clusters = source_emb.shape[2]
    n_dom, n_feat = lax.axis_size("dom"), lax.axis_size("feat")
    share = clusters // n_dom
    tiles, kb, tile, _ = adj_tiles.shape
    me, feat = lax.axis_index("dom"), lax.axis_index("feat")
    meta = jnp.stack([me.astype(jnp.int32), valid_rows[0], feat.astype(jnp.int32)])
    ids = cluster_of[None, :]
    total = channels * n_feat
    outputs = 3 * channels
    sds = jax.ShapeDtypeStruct

    kept, sent = call(
        functools.partial(sums_kernel, share),
        [
            sds((n_dom // 2, channels + COUNT_ROWS, share), F32),
            sds((n_dom // 2, channels + COUNT_ROWS, share), BF),
        ],
        [meta, state, ids],
        [pltpu.VMEM((channels + COUNT_ROWS, rows), BF)],
        flops=2 * channels * rows * clusters * 3,
        bytes_accessed=8 * channels * rows,
    )
    line = n_feat == 4
    sent, state_far = lax.optimization_barrier((sent, state))
    far = [swap(state_far, "feat", k) for k in range(2, n_feat) if k == 2 or not line]
    pieces = call(
        pair_kernel,
        [sds((channels + COUNT_ROWS, share), F32)]
        + [sds((channels + COUNT_ROWS, share), BF)] * (n_dom // 2 - 1),
        [kept, swap(sent, "dom", 1)],
    )
    pieces, state_near, source_emb, target_emb = lax.optimization_barrier(
        (pieces, state, source_emb, target_emb)
    )
    arrived = [pieces[0]] + [swap(pieces[e], "dom", 2 * e) for e in range(1, n_dom // 2)]
    blocks = [state, swap(state_near, "feat", 1)] + far
    pad = [(0, 0), (0, -source_emb.shape[1] % 16), (0, 0)]
    source = lax.dynamic_slice_in_dim(source_emb, me * share, share, 2)
    weights = call(
        functools.partial(weights_kernel, share),
        sds((source.shape[0], clusters, share), BF),
        [jnp.pad(source, pad), jnp.pad(target_emb, pad)],
        flops=source.shape[0] * clusters * share * 4000,
    )
    arrived, weights = lax.optimization_barrier((arrived, weights))
    pooled, values = call(
        functools.partial(pool_kernel, n_dom // 2),
        [sds((channels, share), F32), sds((channels, share), BF)],
        [w_value] + arrived,
    )
    every_value = lax.all_gather(values, "dom", axis=0)
    own_coarse = call(attend_kernel, sds((channels, share), BF), [every_value, weights, pooled])

    own_coarse, w_gates, adj_cols, w_input, coarse_cols = lax.optimization_barrier(
        (own_coarse, w_gates, adj_cols, w_input, coarse_cols)
    )
    coarse_blocks = [own_coarse] + [swap(own_coarse, "feat", k) for k in range(1, n_feat)]
    if line:
        own_coarse, blocks[1:3], state_inner = lax.optimization_barrier(
            (own_coarse, blocks[1:3], state)
        )
        outer = lax.ppermute(blocks[2], "feat", [(1, 0), (2, 3)])
        blocks += [lax.ppermute(state_inner, "feat", [(1, 2), (2, 1)]), outer]
    w = jnp.transpose(w_gates, (2, 0, 1, 3)).reshape(4, outputs, total)
    w_own, w_coarse = w[:3], w[3]
    edge_shape = sds((3 * tile // 2, 2 * tile), BF)
    terms = jnp.concatenate(
        [w_input.reshape(outputs, -1).astype(F32), bias.reshape(outputs, 1)], axis=1
    )
    band, edge_last, edge_first, terms = call(
        band_kernel,
        [sds((tiles, 3 * tile, tile), BF), edge_shape, edge_shape, sds(terms.shape, F32)],
        [meta, adj_cols.reshape(-1), adj_tiles, terms],
        [pltpu.VMEM((3 * tile, tile), F32)],
        flops=10**9,
    )
    coarse_at = coarse_cols.T
    ready = (w_own, w_coarse, band, terms, coarse_at)
    coarse_blocks, ready = lax.optimization_barrier((coarse_blocks, ready))
    w_own, w_coarse, band, terms, coarse_at = ready
    message = sds((total + 3 * tile // 2, 2 * tile), BF)
    last, first = call(
        functools.partial(edge_kernel, n_feat, tile),
        [message, message],
        [meta] + blocks + [edge_last, edge_first],
    )
    folded = call(
        functools.partial(fold_kernel, n_feat),
        sds((outputs, share), BF),
        [meta] + coarse_blocks + [w_coarse],
        [pltpu.VMEM((total, share), BF)],
    )
    given, places, last, first = gather_dom(folded, last, first)
    up = [(i, (i + 1) % n_dom) for i in range(n_dom)]
    left = lax.ppermute(last, "dom", up)
    right = lax.ppermute(first, "dom", [(j, i) for i, j in up])
    pair = 2 * tile
    middle, state_rim, one_rim = call(
        functools.partial(inner_kernel, n_feat, tile),
        [sds((outputs, rows - 2 * pair), F32)] + [sds((total, 2 * pair), BF)] * 2,
        [meta] + blocks + [band, w_own],
        [pltpu.VMEM((total, rows), BF), pltpu.VMEM((total, rows - pair), BF)],
        flops=(4 * total * rows * kb * tile + 6 * total * rows * outputs) // 1,
        bytes_accessed=8 * total * rows,
    )
    rim = call(
        functools.partial(rim_kernel, tile),
        sds((outputs, 2 * pair), F32),
        [left, right, state_rim, one_rim, band, w_own],
        flops=30 * total * rows * outputs,
        bytes_accessed=total * rows,
    )
    return call(
        functools.partial(final_kernel, places, len(given), share, tile),
        sds((channels, rows), BF),
        [meta, coarse_at]
        + given
        + [coarse_tiles, ids, middle, rim, terms, inputs, state],
        [pltpu.VMEM((outputs, clusters), BF)] * 2,
        flops=2 * outputs * rows * clusters,
        bytes_accessed=8 * outputs * rows,
    )


def solution(mesh):
    return jax.shard_map(
        body,
        mesh=mesh,
        in_specs=(
            P("feat", "dom"),
            P(None, "dom"),
            P("dom", None, None, None),
            P("dom", None),
            P("dom"),
            P("dom"),
            P(None, "feat", None, None),
            P(None, "feat", None),
            P(None, "feat"),
            P("feat", None, None),
            P("feat", None, None),
            P("feat", None, None),
            P(),
            P(),
        ),
        out_specs=P("feat", "dom"),
        check_vma=False,
    )
```
